32 devices in a mesh: dom: 8 (over z, x), chan: 4 (over y, core).
Axes of the slice: x: 2, y: 2, z: 4, core: 2. Of those that a mesh axis runs over, the one named last changes fastest.
Arguments:
- latent: bfloat16 [512, 16384], P('chan', 'dom'), may hold values from -6 to 6
- edge_weight: bfloat16 [1024, 128, 128], P('dom'), may hold values from -0.125 to 0.125
- send_blocks: int32 [64, 2], P('dom'), may hold values from 0 to 15, as said below
- send_counts: int32 [64], P('dom'), may hold values from 1 to 2, as said below
- edge_src: int32 [1024], P('dom'), may hold values from 0 to 31, as said below
- edge_obs: int32 [1024], P('dom'), may hold values from 0 to 7, as said below
- w_in: bfloat16 [512, 2048], P('chan'), may hold values from -0.25 to 0.25
- bias: float32 [2048], replicated, may hold values from -3 to 3
- w_out: bfloat16 [2048, 128], replicated, may hold values from -0.125 to 0.125
- g_out: bfloat16 [8192, 128], P('dom'), may hold values from -6 to 6
Outputs:
- obs_out: bfloat16 [8192, 128], P('dom')
- d_latent: bfloat16 [512, 16384], P('chan', 'dom')
The draws below stay inside these ranges and needn't reach their ends.
Inputs may be any that keep to these rules, and one draw needn't show every extreme that they name: `send_counts`: for every sending partition, some receiving partition gets all 2 slots live. `send_blocks`: A mesh block of the sending partition for each slot; entries of slots that are not live are arbitrary. `edge_src`: values below 16 name a mesh block of the partition itself; 16 + p * 2 + s names slot s from partition p to this partition, and only live slots are named. `edge_obs`: every observation block of a partition has at least one edge block.
All inputs are finite; a program needn't handle non-finite values.
Results may differ from the reference program's by a relative error of at most 0.0065.
Values may be sent and summed in bfloat16 or wider, within the bound.
No kernel may reach another device: no remote copies, remote signals or barrier semaphores. Data moves between devices by JAX's collectives and lax.ppermute only.
A program may use at most 64 MiB of HBM per device.

```python
import jax
import jax.numpy as jnp
from jax import lax

D = 512
FF = 2048
OUT = 128
BLK = 128
CAP = 2
NB_DEV = 16
OB_DEV = 8
EB_DEV = 128
NODES = 16384
OBS = 8192
EDGES = 1024
N_DOM = 8


def shared_tables(key):
    subkeys = jax.random.split(key, 9)
    parts_range = jnp.arange(N_DOM)
    counts = jax.random.randint(subkeys[0], (N_DOM, N_DOM), 1, CAP + 1)
    full_at = jax.random.randint(subkeys[1], (N_DOM,), 0, N_DOM)
    counts = jnp.where(parts_range[None, :] == full_at[:, None], CAP, counts)
    single_at = (full_at[0] + 1) % N_DOM
    counts = jnp.where((parts_range[:, None] == 0) & (parts_range[None, :] == single_at), 1, counts)
    blocks = jax.random.randint(subkeys[2], (N_DOM, N_DOM, CAP), 0, NB_DEV)
    slot_range = jnp.arange(CAP)
    first_pair = (parts_range[:, None, None] == 0) & (parts_range[None, :, None] == full_at[0])
    blocks = jnp.where(first_pair & (slot_range[None, None, :] == 0), 0, blocks)
    blocks = jnp.where(first_pair & (slot_range[None, None, :] == CAP - 1), NB_DEV - 1, blocks)
    source = jax.random.randint(subkeys[3], (N_DOM, EB_DEV), 0, N_DOM)
    local_pick = jax.random.randint(subkeys[4], (N_DOM, EB_DEV), 0, 3) == 0
    live_count = counts[source, parts_range[:, None]]
    slot_pick = jax.random.randint(subkeys[5], (N_DOM, EB_DEV), 0, 1048576) % live_count
    local_block = jax.random.randint(subkeys[6], (N_DOM, EB_DEV), 0, NB_DEV)
    sources = jnp.where(local_pick, local_block, NB_DEV + source * CAP + slot_pick)
    edge_range = jnp.arange(EB_DEV)
    top_part = full_at[N_DOM - 1]
    low_part = (top_part + 1) % N_DOM
    sources = jnp.where((parts_range[:, None] == top_part) & (edge_range[None, :] == EB_DEV - 1), NB_DEV + N_DOM * CAP - 1, sources)
    sources = jnp.where((parts_range[:, None] == low_part) & (edge_range[None, :] == 0), 0, sources)
    obs_pick = jax.random.randint(subkeys[7], (N_DOM, EB_DEV), 0, OB_DEV)
    position = edge_range[None, :]
    obs_pick = jnp.where(position < OB_DEV, position, obs_pick)
    row_keys = jax.random.split(subkeys[8], N_DOM)
    obs_pick = jax.vmap(lambda row_key, row: jax.random.permutation(row_key, row))(row_keys, obs_pick)
    return (counts.reshape(N_DOM * N_DOM).astype(jnp.int32), blocks.reshape(N_DOM * N_DOM, CAP).astype(jnp.int32), sources.reshape(N_DOM * EB_DEV).astype(jnp.int32), obs_pick.reshape(N_DOM * EB_DEV).astype(jnp.int32))


def draw_send_counts(key, part):
    tables = shared_tables(key)
    return tables[0]


def draw_send_blocks(key, part):
    tables = shared_tables(key)
    return tables[1]


def draw_edge_src(key, part):
    tables = shared_tables(key)
    return tables[2]


def draw_edge_obs(key, part):
    tables = shared_tables(key)
    return tables[3]


def level_of(stream_key, shape, cuts, least, largest):
    gain = 1.0
    for axis_at, parts in cuts:
        draws = jax.random.uniform(jax.random.fold_in(jax.random.fold_in(stream_key, 6), axis_at), (parts,), jnp.float32, least / len(cuts), largest / len(cuts))
        gain = gain * jnp.repeat(jnp.exp(draws), shape[axis_at] // parts).reshape((-1,) + (1,) * (len(shape) - 1 - axis_at))
    return gain


def normal_values(stream_key, shape, spread, limit, shards=(), dtype=jnp.bfloat16):
    result = spread * jax.random.normal(stream_key, shape, jnp.float32)
    if shards:
        result = result * level_of(stream_key, shape, shards, -0.22, 0.18)
    return jnp.clip(result, -limit, limit).astype(dtype)


def setup_inputs(seed: int = 0) -> dict:
    splits = jax.random.split(jax.random.key(seed), 11)
    latent = normal_values(splits[0], (D, NODES), 1.0, 6.0, ((0, 4), (1, 8)))
    edge_weight = normal_values(splits[1], (EDGES, BLK, BLK), (BLK * EB_DEV // OB_DEV) ** -0.5, 0.125, ((0, 8),))
    send_blocks = draw_send_blocks(jax.random.fold_in(splits[10], 71), 0)
    send_counts = draw_send_counts(jax.random.fold_in(splits[10], 71), 0)
    edge_src = draw_edge_src(jax.random.fold_in(splits[10], 71), 0)
    edge_obs = draw_edge_obs(jax.random.fold_in(splits[10], 71), 0)
    w_in = normal_values(splits[6], (D, FF), D ** -0.5, 0.25, ((0, 4),))
    bias = normal_values(splits[7], (FF,), 0.5, 3.0, (), jnp.float32)
    w_out = normal_values(splits[8], (FF, OUT), FF ** -0.5, 0.125)
    g_out = normal_values(splits[9], (OBS, OUT), 1.0, 6.0, ((0, 8),))
    return dict(latent=latent, edge_weight=edge_weight, send_blocks=send_blocks, send_counts=send_counts, edge_src=edge_src, edge_obs=edge_obs, w_in=w_in, bias=bias, w_out=w_out, g_out=g_out)


def reference(latent, edge_weight, send_blocks, send_counts, edge_src, edge_obs, w_in, bias, w_out, g_out):
    highest = lax.Precision.HIGHEST
    pool_size = NB_DEV + N_DOM * CAP
    node_blocks = latent.reshape(D, N_DOM, NB_DEV, BLK).transpose(1, 2, 0, 3)
    send_table = send_blocks.reshape(N_DOM, N_DOM, CAP)
    live_mask = jnp.arange(CAP)[None, None, :] < send_counts.reshape(N_DOM, N_DOM)[:, :, None]
    weight_blocks = edge_weight.reshape(N_DOM, EB_DEV, BLK, BLK)
    source_table = edge_src.reshape(N_DOM, EB_DEV)
    target_table = edge_obs.reshape(N_DOM, EB_DEV)
    senders = jnp.arange(N_DOM)[:, None]

    def forward_one(device):
        resident = node_blocks[device]
        slot_rows = node_blocks[senders, send_table[:, device, :]]
        slot_rows = jnp.where(live_mask[:, device, :, None, None], slot_rows, jnp.zeros_like(slot_rows))
        source_pool = jnp.concatenate([resident, slot_rows.reshape(N_DOM * CAP, D, BLK)], axis=0)
        picked = source_pool[source_table[device]]
        partial_value = jnp.einsum("edn,eon->edo", picked.astype(jnp.float32), weight_blocks[device].astype(jnp.float32), precision=highest)
        return jax.ops.segment_sum(partial_value, target_table[device], OB_DEV).astype(jnp.bfloat16)

    aggregate = lax.map(forward_one, jnp.arange(N_DOM))
    agg_rows = aggregate.transpose(0, 1, 3, 2).reshape(N_DOM * OB_DEV * BLK, D)
    pre_act = jnp.dot(agg_rows, w_in, preferred_element_type=jnp.float32) + bias[None, :]
    hidden = jax.nn.silu(pre_act).astype(jnp.bfloat16)
    obs_out = jnp.dot(hidden, w_out, preferred_element_type=jnp.float32).astype(jnp.bfloat16)
    back_hidden = jnp.dot(g_out, w_out.T, preferred_element_type=jnp.float32)
    sigma_pre = jax.nn.sigmoid(pre_act)
    grad_pre = (back_hidden * sigma_pre * (1.0 + pre_act * (1.0 - sigma_pre))).astype(jnp.bfloat16)
    grad_agg = jnp.dot(grad_pre, w_in.T, preferred_element_type=jnp.float32).astype(jnp.bfloat16)
    grad_agg = grad_agg.reshape(N_DOM, OB_DEV, BLK, D).transpose(0, 1, 3, 2)

    def backward_one(grad_nodes, device):
        grad_rows = grad_agg[device][target_table[device]]
        grad_picked = jnp.einsum("edo,eon->edn", grad_rows.astype(jnp.float32), weight_blocks[device].astype(jnp.float32), precision=highest)
        pool_grad = jax.ops.segment_sum(grad_picked, source_table[device], pool_size)
        grad_nodes = grad_nodes.at[device].add(pool_grad[:NB_DEV])
        rounded = lax.optimization_barrier(pool_grad[NB_DEV:].astype(jnp.bfloat16))
        slot_grad = rounded.astype(jnp.float32).reshape(N_DOM, CAP, D, BLK)
        slot_grad = jnp.where(live_mask[:, device, :, None, None], slot_grad, jnp.zeros_like(slot_grad))
        grad_nodes = grad_nodes.at[senders, send_table[:, device, :]].add(slot_grad)
        return grad_nodes, None

    start_grad = jnp.zeros((N_DOM, NB_DEV, D, BLK), jnp.float32)
    grad_nodes, unused = lax.scan(backward_one, start_grad, jnp.arange(N_DOM))
    d_latent = grad_nodes.transpose(2, 0, 1, 3).reshape(D, N_DOM * NB_DEV * BLK).astype(jnp.bfloat16)
    return obs_out, d_latent
```

```python
import functools

import jax
import jax.numpy as jnp
from jax import lax
from jax.experimental import pallas as pl
from jax.experimental.pallas import tpu as pltpu
from jax.sharding import PartitionSpec as P

F32 = jnp.float32
BF16 = jnp.bfloat16
UNROLL = 8
NT = (((1,), (1,)), ((), ()))
NN = (((1,), (0,)), ((), ()))


def target(index, shift, count):
    if count & (count - 1) == 0:
        return index ^ shift
    return (index + shift) % count


def source(index, shift, count):
    if count & (count - 1) == 0:
        return index ^ shift
    return (index + count - shift) % count


def send(value, axis, shift, count):
    return lax.ppermute(value, axis, [(i, target(i, shift, count)) for i in range(count)])


def send_back(value, axis, shift, count):
    return lax.ppermute(value, axis, [(target(i, shift, count), i) for i in range(count)])


def vmem(count):
    return [pl.BlockSpec(memory_space=pltpu.VMEM)] * count


def smem(count):
    return [pl.BlockSpec(memory_space=pltpu.SMEM)] * count


def params():
    return pltpu.CompilerParams(vmem_limit_bytes=48 * 1024 * 1024)


def pack_kernel(dom, cap, blk, nodes, blocks_ref, counts_ref, latent_ref, *outs):
    me = lax.axis_index("dom")
    for d in range(dom):
        q = target(me, d, dom)
        for s in range(cap):
            block = jnp.clip(blocks_ref[q, s], 0, nodes - 1)
            start = pl.multiple_of(block * blk, blk)
            live = s < counts_ref[q]

            @pl.when(live)
            def _():
                outs[d][s] = latent_ref[:, pl.ds(start, blk)]

            @pl.when(jnp.logical_not(live))
            def _():
                outs[d][s] = jnp.zeros_like(outs[d][s])


def edge_loop(first, last, body):
    def step(t, carry):
        for u in range(UNROLL):
            i = first + t * UNROLL + u
            body(i, i < last)
        return carry

    lax.fori_loop(0, (last - first + UNROLL - 1) // UNROLL, step, 0)


def local_forward_kernel(
    edges, blk, nodes, obs, src_ref, obs_ref, latent_ref, weight_ref, sum_ref, order_ref, split_ref, total
):
    def sort(e, at):
        near, far = at
        is_near = src_ref[e] < nodes
        order_ref[jnp.where(is_near, near, far)] = e
        step = is_near.astype(jnp.int32)
        return near + step, far - (1 - step)

    near, _ = lax.fori_loop(0, edges, sort, (jnp.int32(0), jnp.int32(edges - 1)), unroll=8)
    split_ref[0] = near
    total[...] = jnp.zeros_like(total)

    def body(i, valid):
        e = order_ref[jnp.minimum(i, edges - 1)]
        start = pl.multiple_of(jnp.minimum(src_ref[e], nodes - 1) * blk, blk)
        term = lax.dot_general(
            weight_ref[e], latent_ref[:, pl.ds(start, blk)], NT, preferred_element_type=F32
        )
        at = jnp.where(valid, obs_ref[e], obs)
        total[at] += term

    edge_loop(0, near, body)
    sum_ref[...] = total[:obs]


def slot_forward_kernel(
    edges, dom, chan, cap, nodes, obs, src_ref, obs_ref, order_ref, split_ref, sum_ref, weight_ref, *rest
):
    arrived, outs, (pool, total) = rest[:dom], rest[dom : dom + chan], rest[dom + chan :]
    me = lax.axis_index("dom")
    for d in range(dom):
        pool[pl.ds(source(me, d, dom) * cap, cap)] = arrived[d][...]
    total[:obs] = sum_ref[...]

    def body(i, valid):
        e = order_ref[jnp.minimum(i, edges - 1)]
        slot = jnp.maximum(src_ref[e] - nodes, 0)
        term = lax.dot_general(weight_ref[e], pool[slot], NT, preferred_element_type=F32)
        at = jnp.where(valid, obs_ref[e], obs)
        total[at] += term

    edge_loop(split_ref[0], edges, body)
    whole = total.reshape((obs + 1) * total.shape[1], total.shape[2])
    rows = outs[0].shape[0]
    mine = lax.axis_index("chan")
    for d in range(chan):
        start = pl.multiple_of(target(mine, d, chan) * rows, rows)
        outs[d][...] = whole[pl.ds(start, rows), :].astype(BF16)


def mlp_kernel(chan, tile, bias_ref, w_out_ref, g_ref, *rest):
    shares, weights = rest[:chan], rest[chan : 2 * chan]
    obs_ref, outs, (full_w, full_a, grad) = (
        rest[2 * chan],
        rest[2 * chan + 1 : 3 * chan + 1],
        rest[3 * chan + 1 :],
    )
    rows, feat = shares[0].shape
    hidden_width = grad.shape[1]
    for d in range(chan):
        full_w[d * feat : (d + 1) * feat, :] = weights[d][...]
        full_a[:, d * feat : (d + 1) * feat] = shares[d][...]
    mine = lax.axis_index("chan")
    g = g_ref[pl.ds(pl.multiple_of(mine * rows, rows), rows), :]
    out = jnp.zeros(obs_ref.shape, F32)
    for h in range(0, hidden_width, tile):
        cols = slice(h, h + tile)
        pre = lax.dot_general(full_a[...], full_w[:, cols], NN, preferred_element_type=F32)
        pre = pre + bias_ref[:, cols]
        sig = 0.5 * jnp.tanh(0.5 * pre) + 0.5
        hidden = (pre * sig).astype(BF16)
        w_out = w_out_ref[cols, :]
        out += lax.dot_general(hidden, w_out, NN, preferred_element_type=F32)
        back = lax.dot_general(g, w_out, NT, preferred_element_type=F32)
        grad[:, cols] = (back * sig * (1.0 + pre * (1.0 - sig))).astype(BF16)
    obs_ref[...] = out.astype(BF16)
    grad_agg = lax.dot_general(full_w[...], grad[...], NT, preferred_element_type=F32)
    for d in range(chan):
        outs[d][...] = grad_agg[d * feat : (d + 1) * feat].astype(BF16)


def gather_grad(chan, per, blk, shares, rows_grad):
    mine = lax.axis_index("chan")
    rows = shares[0].shape[1]
    for d in range(chan):
        start = target(mine, d, chan)
        if rows >= blk:
            for k in range(per):
                rows_grad[start * per + k] = shares[d][:, k * blk : (k + 1) * blk]
        else:
            split = blk // rows
            for k in range(split):

                @pl.when(start % split == k)
                def _():
                    rows_grad[start // split, :, k * rows : (k + 1) * rows] = shares[d][...]


def slot_backward_kernel(
    edges, dom, chan, cap, blk, nodes, obs, src_ref, obs_ref, order_ref, split_ref, weight_ref, *rest
):
    shares, outs, (rows_grad, total) = rest[:chan], rest[chan : chan + dom], rest[chan + dom :]
    gather_grad(chan, max(1, obs // chan), blk, shares, rows_grad)
    total[...] = jnp.zeros_like(total)

    def body(i, valid):
        e = order_ref[jnp.minimum(i, edges - 1)]
        term = lax.dot_general(rows_grad[obs_ref[e]], weight_ref[e], NN, preferred_element_type=F32)
        at = jnp.where(valid, jnp.maximum(src_ref[e] - nodes, 0), dom * cap)
        total[at] += term

    edge_loop(split_ref[0], edges, body)
    me = lax.axis_index("dom")
    for d in range(dom):
        outs[d][...] = total[pl.ds(source(me, d, dom) * cap, cap)].astype(BF16)


def local_backward_kernel(
    edges, chan, blk, nodes, obs, src_ref, obs_ref, order_ref, split_ref, weight_ref, *rest
):
    shares, (out_ref, rows_grad, total) = rest[:chan], rest[chan:]
    gather_grad(chan, max(1, obs // chan), blk, shares, rows_grad)
    total[...] = jnp.zeros_like(total)

    def body(i, valid):
        e = order_ref[jnp.minimum(i, edges - 1)]
        term = lax.dot_general(rows_grad[obs_ref[e]], weight_ref[e], NN, preferred_element_type=F32)
        at = jnp.where(valid, jnp.minimum(src_ref[e], nodes - 1), nodes)
        total[at] += term

    edge_loop(0, split_ref[0], body)
    out_ref[...] = total[:nodes]


def final_kernel(dom, chan, cap, blk, nodes, blocks_ref, counts_ref, local_ref, *rest):
    returned, rows_in = rest[:dom], rest[dom : dom + chan]
    grad_ref, obs_ref, total = rest[dom + chan :]
    me = lax.axis_index("dom")
    total[...] = local_ref[...]
    for d in range(dom):
        q = target(me, d, dom)
        for s in range(cap):

            @pl.when(s < counts_ref[q])
            def _():
                total[jnp.clip(blocks_ref[q, s], 0, nodes - 1)] += returned[d][s].astype(F32)

    for k in range(nodes):
        grad_ref[:, k * blk : (k + 1) * blk] = total[k].astype(BF16)
    mine = lax.axis_index("chan")
    rows = rows_in[0].shape[0]
    for d in range(chan):
        start = pl.multiple_of(source(mine, d, chan) * rows, rows)
        obs_ref[pl.ds(start, rows), :] = rows_in[d][...]


def gather_weights(w_in, chan):
    if chan & (chan - 1):
        return [w_in] + [send(w_in, "chan", d, chan) for d in range(1, chan)]
    weights = {0: w_in}
    bit = chan // 2
    while bit:
        for d in sorted(weights):
            weights[d | bit] = send(weights[d], "chan", bit, chan)
        bit //= 2
    return [weights[d] for d in range(chan)]


def on_device(
    latent, edge_weight, send_blocks, send_counts, edge_src, edge_obs, w_in, bias, w_out, g_out
):
    dom = lax.axis_size("dom")
    chan = lax.axis_size("chan")
    feat, cols = latent.shape
    edges, blk, _ = edge_weight.shape
    nodes = cols // blk
    cap = send_blocks.shape[1]
    obs_rows, out_width = g_out.shape
    obs = obs_rows // blk
    rows = obs_rows // chan
    hidden_width = w_in.shape[1]
    shape = jax.ShapeDtypeStruct

    outgoing = pl.pallas_call(
        functools.partial(pack_kernel, dom, cap, blk, nodes),
        out_shape=[shape((cap, feat, blk), BF16)] * dom,
        in_specs=smem(2) + vmem(1),
        out_specs=vmem(dom),
        compiler_params=params(),
        name="pack",
    )(send_blocks, send_counts, latent)
    arrived = [outgoing[0]] + [send(outgoing[d], "dom", d, dom) for d in range(1, dom)]
    weights = gather_weights(w_in, chan)

    local_sum, order, split = pl.pallas_call(
        functools.partial(local_forward_kernel, edges, blk, nodes, obs),
        out_shape=[
            shape((obs, blk, feat), F32),
            shape((edges,), jnp.int32),
            shape((1,), jnp.int32),
        ],
        in_specs=smem(2) + vmem(2),
        out_specs=vmem(1) + smem(2),
        scratch_shapes=[pltpu.VMEM((obs + 1, blk, feat), F32)],
        compiler_params=params(),
        name="local_forward",
    )(edge_src, edge_obs, latent, edge_weight)

    shares = pl.pallas_call(
        functools.partial(slot_forward_kernel, edges, dom, chan, cap, nodes, obs),
        out_shape=[shape((rows, feat), BF16)] * chan,
        in_specs=smem(4) + vmem(2 + dom),
        out_specs=vmem(chan),
        scratch_shapes=[
            pltpu.VMEM((dom * cap, feat, blk), BF16),
            pltpu.VMEM((obs + 1, blk, feat), F32),
        ],
        compiler_params=params(),
        name="slot_forward",
    )(edge_src, edge_obs, order, split, local_sum, edge_weight, *arrived)
    shares = [shares[0]] + [send(shares[d], "chan", d, chan) for d in range(1, chan)]

    mlp = pl.pallas_call(
        functools.partial(mlp_kernel, chan, min(512, hidden_width)),
        out_shape=[shape((rows, out_width), BF16)] + [shape((feat, rows), BF16)] * chan,
        in_specs=vmem(3 + 2 * chan),
        out_specs=vmem(1 + chan),
        scratch_shapes=[
            pltpu.VMEM((chan * feat, hidden_width), BF16),
            pltpu.VMEM((rows, chan * feat), BF16),
            pltpu.VMEM((rows, hidden_width), BF16),
        ],
        compiler_params=params(),
        name="mlp",
    )(bias.reshape(1, hidden_width), w_out, g_out, *shares, *weights)
    obs_part, grads = mlp[0], mlp[1:]
    grads = [grads[0]] + [send_back(grads[d], "chan", d, chan) for d in range(1, chan)]
    obs_parts = [obs_part] + [send(obs_part, "chan", d, chan) for d in range(1, chan)]

    slot_grads = pl.pallas_call(
        functools.partial(slot_backward_kernel, edges, dom, chan, cap, blk, nodes, obs),
        out_shape=[shape((cap, feat, blk), BF16)] * dom,
        in_specs=smem(4) + vmem(1 + chan),
        out_specs=vmem(dom),
        scratch_shapes=[
            pltpu.VMEM((obs, feat, blk), BF16),
            pltpu.VMEM((dom * cap + 1, feat, blk), F32),
        ],
        compiler_params=params(),
        name="slot_backward",
    )(edge_src, edge_obs, order, split, edge_weight, *grads)
    returned = [slot_grads[0]] + [
        send_back(slot_grads[d], "dom", d, dom) for d in range(1, dom)
    ]

    local_grad = pl.pallas_call(
        functools.partial(local_backward_kernel, edges, chan, blk, nodes, obs),
        out_shape=shape((nodes, feat, blk), F32),
        in_specs=smem(4) + vmem(1 + chan),
        out_specs=pl.BlockSpec(memory_space=pltpu.VMEM),
        scratch_shapes=[
            pltpu.VMEM((obs, feat, blk), BF16),
            pltpu.VMEM((nodes + 1, feat, blk), F32),
        ],
        compiler_params=params(),
        name="local_backward",
    )(edge_src, edge_obs, order, split, edge_weight, *grads)

    d_latent, obs_out = pl.pallas_call(
        functools.partial(final_kernel, dom, chan, cap, blk, nodes),
        out_shape=[shape((feat, cols), BF16), shape((obs_rows, out_width), BF16)],
        in_specs=smem(2) + vmem(1 + dom + chan),
        out_specs=vmem(2),
        scratch_shapes=[pltpu.VMEM((nodes, feat, blk), F32)],
        compiler_params=params(),
        name="final",
    )(send_blocks, send_counts, local_grad, *returned, *obs_parts)
    return obs_out, d_latent


def solution(mesh):
    return jax.shard_map(
        on_device,
        mesh=mesh,
        in_specs=(
            P("chan", "dom"),
            P("dom", None, None),
            P("dom", None),
            P("dom"),
            P("dom"),
            P("dom"),
            P("chan", None),
            P(),
            P(),
            P("dom", None),
        ),
        out_specs=(P("dom", None), P("chan", "dom")),
        check_vma=False,
    )
```

```python
import functools

import jax
import jax.numpy as jnp
from jax import lax
from jax.experimental import pallas as pl
from jax.experimental.pallas import tpu as pltpu
from jax.sharding import PartitionSpec as P

F32 = jnp.float32
BF16 = jnp.bfloat16
UNROLL = 32
NT = (((1,), (1,)), ((), ()))
NN = (((1,), (0,)), ((), ()))


def target(index, shift, count):
    if count & (count - 1) == 0:
        return index ^ shift
    return (index + shift) % count


def source(index, shift, count):
    if count & (count - 1) == 0:
        return index ^ shift
    return (index + count - shift) % count


def send(value, axis, shift, count):
    return lax.ppermute(value, axis, [(i, target(i, shift, count)) for i in range(count)])


def send_back(value, axis, shift, count):
    return lax.ppermute(value, axis, [(target(i, shift, count), i) for i in range(count)])


def vmem(count):
    return [pl.BlockSpec(memory_space=pltpu.VMEM)] * count


def smem(count):
    return [pl.BlockSpec(memory_space=pltpu.SMEM)] * count


def hbm(count):
    return [pl.BlockSpec(memory_space=pltpu.HBM)] * count


def params():
    return pltpu.CompilerParams(vmem_limit_bytes=48 * 1024 * 1024)


def is_near(shift, dom):
    return shift < (dom + 1) // 2


def fetch(pairs, sems):
    copies = [pltpu.make_async_copy(a, b, sems.at[i]) for i, (a, b) in enumerate(pairs)]
    for copy in copies:
        copy.start()
    return copies


def pack_kernel(dom, cap, blk, nodes, blocks_hbm, counts_hbm, latent_hbm, *rest):
    outs, (blocks_ref, counts_ref, latent_ref, sems) = rest[:dom], rest[dom:]
    pairs = ((latent_hbm, latent_ref), (blocks_hbm, blocks_ref), (counts_hbm, counts_ref))
    for copy in fetch(pairs, sems):
        copy.wait()
    me = lax.axis_index("dom")
    for d in range(dom):
        q = target(me, d, dom)
        for s in range(cap):
            block = jnp.clip(blocks_ref[s, q], 0, nodes - 1)
            value = latent_ref[:, pl.ds(pl.multiple_of(block * blk, blk), blk)]
            outs[d][s] = jnp.where(s < counts_ref[q], value, jnp.zeros_like(value))


class Plan:
    def __init__(self, edges):
        self.edges = edges
        self.length = edges + UNROLL

    def size(self):
        return 9 * self.length + 3

    def at(self, kind, field):
        return (kind * 3 + field) * self.length

    def make(self, ref, src_ref, obs_ref, nodes, obs, dom, cap):
        me = lax.axis_index("dom")
        near_of = [
            functools.reduce(
                jnp.logical_or, [source(me, d, dom) == p for d in range(dom) if is_near(d, dom)]
            ).astype(jnp.int32)
            for p in range(dom)
        ]
        near_bits = None
        if dom <= 16:
            near_bits = sum(near_of[p] << p for p in range(dom))

        def one(e, counts):
            src = src_ref[e]
            slot = jnp.maximum(src - nodes, 0)
            p = slot // cap
            if near_bits is not None:
                near = (near_bits >> p) & 1
            else:
                near = is_near(lax.rem(me - p + dom, dom), dom).astype(jnp.int32)
            local = (src < nodes).astype(jnp.int32)
            near = (1 - local) * near
            far = 1 - local - near
            kind = near + 2 * far
            i = local * counts[0] + near * counts[1] + far * counts[2]
            base = kind * 3 * self.length + i
            ref[base] = e
            ref[base + self.length] = jnp.where(local == 1, src, slot)
            ref[base + 2 * self.length] = obs_ref[e]
            return counts[0] + local, counts[1] + near, counts[2] + far

        zero = jnp.int32(0)
        counts = lax.fori_loop(0, self.edges, one, (zero, zero, zero), unroll=4)
        for kind in range(3):
            trash = nodes if kind == 0 else dom * cap
            start = counts[kind]

            def fill(i, carry):
                base = kind * 3 * self.length + start + i
                ref[base] = 0
                ref[base + self.length] = trash
                ref[base + 2 * self.length] = obs
                return carry

            lax.fori_loop(0, UNROLL, fill, 0, unroll=4)
            ref[9 * self.length + kind] = start

    def run(self, ref, kind, body):
        def step(t, carry):
            for u in range(UNROLL):
                i = kind * 3 * self.length + t * UNROLL + u
                body(ref[i], ref[i + self.length], ref[i + 2 * self.length])
            return carry

        count = ref[9 * self.length + kind]
        lax.fori_loop(0, (count + UNROLL - 1) // UNROLL, step, 0)


def local_forward_kernel(
    plan, dom, cap, blk, nodes, obs, src_hbm, obs_hbm, latent_hbm, weight_hbm, sum_ref, plan_ref, weight_ref, *rest
):
    src_ref, obs_ref, latent_ref, pool, sems = rest
    pairs = (
        (src_hbm, src_ref),
        (obs_hbm, obs_ref),
        (latent_hbm, latent_ref),
        (weight_hbm, weight_ref),
    )
    copies = fetch(pairs, sems)
    copies[0].wait()
    copies[1].wait()
    plan.make(plan_ref, src_ref, obs_ref, nodes, obs, dom, cap)
    copies[2].wait()
    for k in range(nodes):
        pool[k] = latent_ref[:, k * blk : (k + 1) * blk].T
    sum_ref[...] = jnp.zeros_like(sum_ref)
    copies[3].wait()

    def body(e, k, j):
        sum_ref[j] += lax.dot_general(weight_ref[e], pool[k], NN, preferred_element_type=F32)

    plan.run(plan_ref, 0, body)


def add_slots(plan, kind, shifts, dom, cap, plan_ref, weight_ref, arrived, pool, total):
    me = lax.axis_index("dom")
    for d, value in zip(shifts, arrived):
        start = source(me, d, dom) * cap
        for s in range(cap):
            pool[start + s] = value[s].T

    def body(e, k, j):
        total[j] += lax.dot_general(weight_ref[e], pool[k], NN, preferred_element_type=F32)

    plan.run(plan_ref, kind, body)


def near_forward_kernel(plan, shifts, dom, cap, plan_ref, sum_ref, weight_ref, *rest):
    arrived, (out_ref, pool) = rest[: len(shifts)], rest[len(shifts) :]
    out_ref[...] = sum_ref[...]
    add_slots(plan, 1, shifts, dom, cap, plan_ref, weight_ref, arrived, pool, out_ref)


def far_forward_kernel(plan, shifts, dom, cap, chan, plan_ref, sum_ref, weight_ref, *rest):
    count = len(shifts)
    arrived, outs, (pool, total) = rest[:count], rest[count : count + chan], rest[count + chan :]
    total[...] = sum_ref[...]
    add_slots(plan, 2, shifts, dom, cap, plan_ref, weight_ref, arrived, pool, total)
    whole = total.reshape(total.shape[0] * total.shape[1], total.shape[2])
    rows = outs[0].shape[0]
    mine = lax.axis_index("chan")
    for d in range(chan):
        start = pl.multiple_of(target(mine, d, chan) * rows, rows)
        outs[d][...] = whole[pl.ds(start, rows), :].astype(BF16)


def mlp_kernel(chan, tile, bias_ref, w_out_ref, g_ref, *rest):
    shares, weights = rest[:chan], rest[chan : 2 * chan]
    obs_ref, outs, (full_w, full_a, grad) = (
        rest[2 * chan],
        rest[2 * chan + 1 : 3 * chan + 1],
        rest[3 * chan + 1 :],
    )
    rows, feat = shares[0].shape
    hidden_width = grad.shape[1]
    for d in range(chan):
        full_w[d * feat : (d + 1) * feat, :] = weights[d][...]
        full_a[:, d * feat : (d + 1) * feat] = shares[d][...]
    mine = lax.axis_index("chan")
    g = g_ref[pl.ds(pl.multiple_of(mine * rows, rows), rows), :]
    out = jnp.zeros(obs_ref.shape, F32)
    for h in range(0, hidden_width, tile):
        cols = slice(h, h + tile)
        pre = lax.dot_general(full_a[...], full_w[:, cols], NN, preferred_element_type=F32)
        pre = pre + bias_ref[:, cols]
        sig = 0.5 * jnp.tanh(0.5 * pre) + 0.5
        hidden = (pre * sig).astype(BF16)
        w_out = w_out_ref[cols, :]
        out += lax.dot_general(hidden, w_out, NN, preferred_element_type=F32)
        back = lax.dot_general(g, w_out, NT, preferred_element_type=F32)
        grad[:, cols] = (back * sig * (1.0 + pre * (1.0 - sig))).astype(BF16)
    obs_ref[...] = out.astype(BF16)
    grad_agg = lax.dot_general(full_w[...], grad[...], NT, preferred_element_type=F32)
    for d in range(chan):
        outs[d][...] = grad_agg[d * feat : (d + 1) * feat].astype(BF16)


def gather_grad(chan, per, blk, shares, rows_grad):
    mine = lax.axis_index("chan")
    rows = shares[0].shape[1]
    for d in range(chan):
        start = target(mine, d, chan)
        if rows >= blk:
            for k in range(per):
                rows_grad[start * per + k] = shares[d][:, k * blk : (k + 1) * blk]
        else:
            split = blk // rows
            for k in range(split):

                @pl.when(start % split == k)
                def _():
                    rows_grad[start // split, :, k * rows : (k + 1) * rows] = shares[d][...]


def slot_gradients(plan, kind, shifts, dom, cap, plan_ref, weight_ref, rows_grad, outs, total):
    total[...] = jnp.zeros_like(total)

    def body(e, k, j):
        total[k] += lax.dot_general(rows_grad[j], weight_ref[e], NN, preferred_element_type=F32)

    plan.run(plan_ref, kind, body)
    me = lax.axis_index("dom")
    for d, out in zip(shifts, outs):
        out[...] = total[pl.ds(source(me, d, dom) * cap, cap)].astype(BF16)


def far_backward_kernel(plan, shifts, dom, cap, chan, blk, obs, plan_ref, weight_ref, *rest):
    shares, rows_grad, (*outs, total) = rest[:chan], rest[chan], rest[chan + 1 :]
    gather_grad(chan, max(1, obs // chan), blk, shares, rows_grad)
    slot_gradients(plan, 2, shifts, dom, cap, plan_ref, weight_ref, rows_grad, outs, total)


def near_backward_kernel(plan, shifts, dom, cap, plan_ref, weight_ref, rows_grad, *rest):
    *outs, total = rest
    slot_gradients(plan, 1, shifts, dom, cap, plan_ref, weight_ref, rows_grad, outs, total)


def local_backward_kernel(plan, plan_ref, weight_ref, rows_grad, total):
    total[...] = jnp.zeros_like(total)

    def body(e, k, j):
        total[k] += lax.dot_general(rows_grad[j], weight_ref[e], NN, preferred_element_type=F32)

    plan.run(plan_ref, 0, body)


def rows_kernel(chan, *rest):
    parts, obs_ref = rest[:chan], rest[chan]
    mine = lax.axis_index("chan")
    rows = parts[0].shape[0]
    for d in range(chan):
        start = pl.multiple_of(source(mine, d, chan) * rows, rows)
        obs_ref[pl.ds(start, rows), :] = parts[d][...]


def final_kernel(dom, cap, blk, nodes, blocks_hbm, counts_hbm, local_ref, *rest):
    returned, (grad_ref, total, blocks_ref, counts_ref, sems) = rest[:dom], rest[dom:]
    copies = fetch(((blocks_hbm, blocks_ref), (counts_hbm, counts_ref)), sems)
    total[...] = local_ref[:nodes]
    for copy in copies:
        copy.wait()
    me = lax.axis_index("dom")
    for d in range(dom):
        q = target(me, d, dom)
        for s in range(cap):
            value = returned[d][s].astype(F32)
            value = jnp.where(s < counts_ref[q], value, jnp.zeros_like(value))
            total[jnp.clip(blocks_ref[s, q], 0, nodes - 1)] += value
    for k in range(nodes):
        grad_ref[:, k * blk : (k + 1) * blk] = total[k].astype(BF16)


def after(value, *others):
    return lax.optimization_barrier((value, *others))[0]


def on_device(
    latent, edge_weight, send_blocks, send_counts, edge_src, edge_obs, w_in, bias, w_out, g_out
):
    dom = lax.axis_size("dom")
    chan = lax.axis_size("chan")
    feat, cols = latent.shape
    edges, blk, _ = edge_weight.shape
    nodes = cols // blk
    cap = send_blocks.shape[1]
    obs_rows, out_width = g_out.shape
    obs = obs_rows // blk
    rows = obs_rows // chan
    hidden_width = w_in.shape[1]
    shape = jax.ShapeDtypeStruct
    plan = Plan(edges)
    near = [d for d in range(dom) if is_near(d, dom)]
    far = [d for d in range(dom) if not is_near(d, dom)]
    tables = (send_blocks.T, send_counts)
    i32 = jnp.int32

    outgoing = pl.pallas_call(
        functools.partial(pack_kernel, dom, cap, blk, nodes),
        out_shape=[shape((cap, feat, blk), BF16)] * dom,
        in_specs=hbm(3),
        out_specs=vmem(dom),
        scratch_shapes=[
            pltpu.SMEM((cap, dom), i32),
            pltpu.SMEM((dom,), i32),
            pltpu.VMEM((feat, cols), BF16),
            pltpu.SemaphoreType.DMA((3,)),
        ],
        compiler_params=params(),
        name="pack",
    )(*tables, latent)
    arrived = {0: outgoing[0]}
    for d in far + near[1:]:
        arrived[d] = send(outgoing[d], "dom", d, dom)

    w_mine = after(w_in, outgoing[0])
    weights = {0: w_mine}
    late = chan // 2 if chan & (chan - 1) == 0 else 0
    if late:
        weights[late] = send(w_mine, "chan", late, chan)
        bit = late // 2
        while bit:
            for d in [d for d in sorted(weights) if d < late]:
                weights[d | bit] = send(weights[d], "chan", bit, chan)
            bit //= 2
    else:
        for d in range(1, chan):
            weights[d] = send(w_mine, "chan", d, chan)

    local_sum, table, weight = pl.pallas_call(
        functools.partial(local_forward_kernel, plan, dom, cap, blk, nodes, obs),
        out_shape=[
            shape((obs + 1, blk, feat), F32),
            shape((plan.size(),), i32),
            shape(edge_weight.shape, BF16),
        ],
        in_specs=hbm(4),
        out_specs=vmem(1) + smem(1) + vmem(1),
        scratch_shapes=[
            pltpu.SMEM((edges,), i32),
            pltpu.SMEM((edges,), i32),
            pltpu.VMEM((feat, cols), BF16),
            pltpu.VMEM((nodes + 1, blk, feat), BF16),
            pltpu.SemaphoreType.DMA((4,)),
        ],
        compiler_params=params(),
        name="local_forward",
    )(edge_src, edge_obs, latent, edge_weight)

    pool = pltpu.VMEM((dom * cap + 1, blk, feat), BF16)
    near_sum = pl.pallas_call(
        functools.partial(near_forward_kernel, plan, near, dom, cap),
        out_shape=shape((obs + 1, blk, feat), F32),
        in_specs=smem(1) + vmem(2 + len(near)),
        out_specs=pl.BlockSpec(memory_space=pltpu.VMEM),
        scratch_shapes=[pool],
        compiler_params=params(),
        name="near_forward",
    )(table, local_sum, weight, *[arrived[d] for d in near])

    shares = pl.pallas_call(
        functools.partial(far_forward_kernel, plan, far, dom, cap, chan),
        out_shape=[shape((rows, feat), BF16)] * chan,
        in_specs=smem(1) + vmem(2 + len(far)),
        out_specs=vmem(chan),
        scratch_shapes=[pool, pltpu.VMEM((obs + 1, blk, feat), F32)],
        compiler_params=params(),
        name="far_forward",
    )(table, near_sum, weight, *[arrived[d] for d in far])
    if late:
        weights[late] = after(weights[late], shares[0])
        bit = late // 2
        while bit:
            for d in [d for d in sorted(weights) if d >= late]:
                weights[d | bit] = send(weights[d], "chan", bit, chan)
            bit //= 2
    shares = [shares[0]] + [send(shares[d], "chan", d, chan) for d in range(1, chan)]

    mlp = pl.pallas_call(
        functools.partial(mlp_kernel, chan, min(512, hidden_width)),
        out_shape=[shape((rows, out_width), BF16)] + [shape((feat, rows), BF16)] * chan,
        in_specs=vmem(3 + 2 * chan),
        out_specs=vmem(1 + chan),
        scratch_shapes=[
            pltpu.VMEM((chan * feat, hidden_width), BF16),
            pltpu.VMEM((rows, chan * feat), BF16),
            pltpu.VMEM((rows, hidden_width), BF16),
        ],
        compiler_params=params(),
        name="mlp",
    )(bias.reshape(1, hidden_width), w_out, g_out, *shares, *[weights[d] for d in range(chan)])
    obs_part, grads = mlp[0], mlp[1:]
    grads = [grads[0]] + [send_back(grads[d], "chan", d, chan) for d in range(1, chan)]

    slots = pltpu.VMEM((dom * cap + 1, feat, blk), F32)
    slot_shape = shape((cap, feat, blk), BF16)
    rows_grad, *far_grads = pl.pallas_call(
        functools.partial(far_backward_kernel, plan, far, dom, cap, chan, blk, obs),
        out_shape=[shape((obs + 1, feat, blk), BF16)] + [slot_shape] * len(far),
        in_specs=smem(1) + vmem(1 + chan),
        out_specs=vmem(1 + len(far)),
        scratch_shapes=[slots],
        compiler_params=params(),
        name="far_backward",
    )(table, weight, *grads)
    returned = {d: send_back(value, "dom", d, dom) for d, value in zip(far, far_grads)}

    near_grads = pl.pallas_call(
        functools.partial(near_backward_kernel, plan, near, dom, cap),
        out_shape=[slot_shape] * len(near),
        in_specs=smem(1) + vmem(2),
        out_specs=vmem(len(near)),
        scratch_shapes=[slots],
        compiler_params=params(),
        name="near_backward",
    )(table, weight, rows_grad)
    returned[0] = near_grads[0]
    for d, value in zip(near[1:], near_grads[1:]):
        returned[d] = send_back(value, "dom", d, dom)

    obs_part = after(obs_part, near_grads[0])
    obs_parts = [obs_part] + [send(obs_part, "chan", d, chan) for d in range(1, chan)]

    local_grad = pl.pallas_call(
        functools.partial(local_backward_kernel, plan),
        out_shape=shape((nodes + 1, feat, blk), F32),
        in_specs=smem(1) + vmem(2),
        out_specs=pl.BlockSpec(memory_space=pltpu.VMEM),
        compiler_params=params(),
        name="local_backward",
    )(table, weight, after(rows_grad, near_grads[0]))

    obs_out = pl.pallas_call(
        functools.partial(rows_kernel, chan),
        out_shape=shape((obs_rows, out_width), BF16),
        in_specs=vmem(chan),
        out_specs=pl.BlockSpec(memory_space=pltpu.VMEM),
        compiler_params=params(),
        name="rows",
    )(*obs_parts)

    d_latent = pl.pallas_call(
        functools.partial(final_kernel, dom, cap, blk, nodes),
        out_shape=shape((feat, cols), BF16),
        in_specs=hbm(2) + vmem(1 + dom),
        out_specs=pl.BlockSpec(memory_space=pltpu.VMEM),
        scratch_shapes=[
            pltpu.VMEM((nodes, feat, blk), F32),
            pltpu.SMEM((cap, dom), i32),
            pltpu.SMEM((dom,), i32),
            pltpu.SemaphoreType.DMA((2,)),
        ],
        compiler_params=params(),
        name="final",
    )(*tables, local_grad, *[returned[d] for d in range(dom)])
    return obs_out, d_latent


def solution(mesh):
    return jax.shard_map(
        on_device,
        mesh=mesh,
        in_specs=(
            P("chan", "dom"),
            P("dom", None, None),
            P("dom", None),
            P("dom"),
            P("dom"),
            P("dom"),
            P("chan", None),
            P(),
            P(),
            P("dom", None),
        ),
        out_specs=(P("dom", None), P("chan", "dom")),
        check_vma=False,
    )
```

```python
import functools

import jax
import jax.numpy as jnp
from jax import lax
from jax.experimental import pallas as pl
from jax.experimental.pallas import tpu as pltpu
from jax.sharding import PartitionSpec as P

F32 = jnp.float32
BF16 = jnp.bfloat16
UNROLL = 32
NT = (((1,), (1,)), ((), ()))
NN = (((1,), (0,)), ((), ()))


def target(index, shift, count):
    if count & (count - 1) == 0:
        return index ^ shift
    return (index + shift) % count


def source(index, shift, count):
    if count & (count - 1) == 0:
        return index ^ shift
    return (index + count - shift) % count


def send(value, axis, shift, count):
    return lax.ppermute(value, axis, [(i, target(i, shift, count)) for i in range(count)])


def send_back(value, axis, shift, count):
    return lax.ppermute(value, axis, [(target(i, shift, count), i) for i in range(count)])


def vmem(count):
    return [pl.BlockSpec(memory_space=pltpu.VMEM)] * count


def smem(count):
    return [pl.BlockSpec(memory_space=pltpu.SMEM)] * count


def hbm(count):
    return [pl.BlockSpec(memory_space=pltpu.HBM)] * count


def in_hbm(*values):
    return [pltpu.with_memory_space_constraint(v, pltpu.HBM) for v in values]


def cost(products):
    return pl.CostEstimate(flops=products * 2**24, bytes_accessed=2**10, transcendentals=0)


def params():
    return pltpu.CompilerParams(vmem_limit_bytes=48 * 1024 * 1024)


def is_near(shift, dom):
    return shift < (dom + 1) // 2


def fetch(pairs, sems):
    copies = [pltpu.make_async_copy(a, b, sems.at[i]) for i, (a, b) in enumerate(pairs)]
    for copy in copies:
        copy.start()
    return copies


def pack_kernel(dom, cap, blk, nodes, blocks_hbm, counts_hbm, latent_hbm, *rest):
    outs, (blocks_ref, counts_ref, latent_ref, sems) = rest[:dom], rest[dom:]
    pairs = ((latent_hbm, latent_ref), (blocks_hbm, blocks_ref), (counts_hbm, counts_ref))
    for copy in fetch(pairs, sems):
        copy.wait()
    me = lax.axis_index("dom")
    for d in range(dom):
        q = target(me, d, dom)
        for s in range(cap):
            block = jnp.clip(blocks_ref[s, q], 0, nodes - 1)
            value = latent_ref[:, pl.ds(pl.multiple_of(block * blk, blk), blk)]
            outs[d][s] = jnp.where(s < counts_ref[q], value, jnp.zeros_like(value))


class Plan:
    def __init__(self, edges):
        self.edges = edges
        self.length = edges + UNROLL

    def size(self):
        return 9 * self.length + 3

    def at(self, kind, field):
        return (kind * 3 + field) * self.length

    def make(self, ref, src_ref, obs_ref, nodes, obs, dom, cap):
        me = lax.axis_index("dom")
        mask = None
        if dom * cap <= 31:
            bits = (1 << cap) - 1
            mask = sum(bits << (source(me, d, dom) * cap) for d in range(dom) if is_near(d, dom))

        def one(e, counts):
            src = src_ref[e]
            slot = jnp.maximum(src - nodes, 0)
            if mask is not None:
                near = lax.shift_right_logical(mask, slot) & 1
            else:
                shift = lax.rem(me - lax.div(slot, cap) + dom, dom)
                near = is_near(shift, dom).astype(jnp.int32)
            local = (src < nodes).astype(jnp.int32)
            near = (1 - local) * near
            far = 1 - local - near
            kind = near + 2 * far
            i = local * counts[0] + near * counts[1] + far * counts[2]
            base = kind * 3 * self.length + i
            ref[base] = e
            ref[base + self.length] = jnp.where(local == 1, src, slot)
            ref[base + 2 * self.length] = obs_ref[e]
            return counts[0] + local, counts[1] + near, counts[2] + far

        zero = jnp.int32(0)
        counts = lax.fori_loop(0, self.edges, one, (zero, zero, zero), unroll=4)
        for kind in range(3):
            trash = nodes if kind == 0 else dom * cap
            start = counts[kind]

            def fill(i, carry):
                base = kind * 3 * self.length + start + i
                ref[base] = 0
                ref[base + self.length] = trash
                ref[base + 2 * self.length] = obs
                return carry

            lax.fori_loop(0, UNROLL, fill, 0, unroll=4)
            ref[9 * self.length + kind] = start

    def run(self, ref, kind, body):
        def step(t, carry):
            for u in range(UNROLL):
                i = kind * 3 * self.length + t * UNROLL + u
                body(ref[i], ref[i + self.length], ref[i + 2 * self.length])
            return carry

        count = ref[9 * self.length + kind]
        lax.fori_loop(0, (count + UNROLL - 1) // UNROLL, step, 0)


def first_forward_kernel(
    plan, shifts, dom, cap, blk, nodes, obs, src_hbm, obs_hbm, latent_hbm, weight_hbm, *rest
):
    count = len(shifts)
    arrived, (sum_ref, plan_ref, weight_ref) = rest[:count], rest[count : count + 3]
    src_ref, obs_ref, latent_ref, pool, slots, sems = rest[count + 3 :]
    pairs = (
        (src_hbm, src_ref),
        (obs_hbm, obs_ref),
        (latent_hbm, latent_ref),
        (weight_hbm, weight_ref),
    )
    copies = fetch(pairs, sems)
    sum_ref[...] = jnp.zeros_like(sum_ref)
    copies[0].wait()
    copies[1].wait()
    plan.make(plan_ref, src_ref, obs_ref, nodes, obs, dom, cap)
    copies[2].wait()
    for k in range(nodes):
        pool[k] = latent_ref[:, k * blk : (k + 1) * blk].T
    copies[3].wait()

    def body(e, k, j):
        sum_ref[j] += lax.dot_general(weight_ref[e], pool[k], NN, preferred_element_type=F32)

    plan.run(plan_ref, 0, body)
    add_slots(plan, 1, shifts, dom, cap, plan_ref, weight_ref, arrived, slots, sum_ref)


def add_slots(plan, kind, shifts, dom, cap, plan_ref, weight_ref, arrived, pool, total):
    me = lax.axis_index("dom")
    for d, value in zip(shifts, arrived):
        start = source(me, d, dom) * cap
        for s in range(cap):
            pool[start + s] = value[s].T

    def body(e, k, j):
        total[j] += lax.dot_general(weight_ref[e], pool[k], NN, preferred_element_type=F32)

    plan.run(plan_ref, kind, body)


def far_forward_kernel(plan, shifts, dom, cap, chan, plan_ref, sum_ref, weight_ref, *rest):
    count = len(shifts)
    arrived, outs, (pool, total) = rest[:count], rest[count : count + chan], rest[count + chan :]
    total[...] = sum_ref[...]
    add_slots(plan, 2, shifts, dom, cap, plan_ref, weight_ref, arrived, pool, total)
    whole = total.reshape(total.shape[0] * total.shape[1], total.shape[2])
    rows = outs[0].shape[0]
    mine = lax.axis_index("chan")
    for d in range(chan):
        start = pl.multiple_of(target(mine, d, chan) * rows, rows)
        outs[d][...] = whole[pl.ds(start, rows), :].astype(BF16)


def mlp_kernel(chan, tile, bias_ref, w_out_ref, g_ref, *rest):
    shares, weights = rest[:chan], rest[chan : 2 * chan]
    obs_ref, outs, (full_w, full_a, grad) = (
        rest[2 * chan],
        rest[2 * chan + 1 : 3 * chan + 1],
        rest[3 * chan + 1 :],
    )
    rows, feat = shares[0].shape
    hidden_width = grad.shape[1]
    for d in range(chan):
        full_w[d * feat : (d + 1) * feat, :] = weights[d][...]
        full_a[:, d * feat : (d + 1) * feat] = shares[d][...]
    mine = lax.axis_index("chan")
    g = g_ref[pl.ds(pl.multiple_of(mine * rows, rows), rows), :]
    out = jnp.zeros(obs_ref.shape, F32)
    for h in range(0, hidden_width, tile):
        cols = slice(h, h + tile)
        pre = lax.dot_general(full_a[...], full_w[:, cols], NN, preferred_element_type=F32)
        pre = pre + bias_ref[:, cols]
        sig = 0.5 * jnp.tanh(0.5 * pre) + 0.5
        hidden = (pre * sig).astype(BF16)
        w_out = w_out_ref[cols, :]
        out += lax.dot_general(hidden, w_out, NN, preferred_element_type=F32)
        back = lax.dot_general(g, w_out, NT, preferred_element_type=F32)
        grad[:, cols] = (back * sig * (1.0 + pre * (1.0 - sig))).astype(BF16)
    obs_ref[...] = out.astype(BF16)
    grad_agg = lax.dot_general(full_w[...], grad[...], NT, preferred_element_type=F32)
    for d in range(chan):
        outs[d][...] = grad_agg[d * feat : (d + 1) * feat].astype(BF16)


def gather_grad(chan, per, blk, shares, rows_grad):
    mine = lax.axis_index("chan")
    rows = shares[0].shape[1]
    for d in range(chan):
        start = target(mine, d, chan)
        if rows >= blk:
            for k in range(per):
                rows_grad[start * per + k] = shares[d][:, k * blk : (k + 1) * blk]
        else:
            split = blk // rows
            for k in range(split):

                @pl.when(start % split == k)
                def _():
                    rows_grad[start // split, :, k * rows : (k + 1) * rows] = shares[d][...]


def slot_gradients(plan, kind, shifts, dom, cap, plan_ref, weight_ref, rows_grad, outs, total):
    total[...] = jnp.zeros_like(total)

    def body(e, k, j):
        total[k] += lax.dot_general(rows_grad[j], weight_ref[e], NN, preferred_element_type=F32)

    plan.run(plan_ref, kind, body)
    me = lax.axis_index("dom")
    for d, out in zip(shifts, outs):
        out[...] = total[pl.ds(source(me, d, dom) * cap, cap)].astype(BF16)


def far_backward_kernel(plan, shifts, dom, cap, chan, blk, obs, plan_ref, weight_ref, *rest):
    shares, rows_grad, (*outs, total) = rest[:chan], rest[chan], rest[chan + 1 :]
    gather_grad(chan, max(1, obs // chan), blk, shares, rows_grad)
    slot_gradients(plan, 2, shifts, dom, cap, plan_ref, weight_ref, rows_grad, outs, total)


def rest_backward_kernel(plan, shifts, dom, cap, plan_ref, weight_ref, rows_grad, *rest):
    *outs, total, slots = rest
    slot_gradients(plan, 1, shifts, dom, cap, plan_ref, weight_ref, rows_grad, outs, slots)
    total[...] = jnp.zeros_like(total)

    def body(e, k, j):
        total[k] += lax.dot_general(rows_grad[j], weight_ref[e], NN, preferred_element_type=F32)

    plan.run(plan_ref, 0, body)


def rows_kernel(chan, *rest):
    parts, obs_ref = rest[:chan], rest[chan]
    mine = lax.axis_index("chan")
    rows = parts[0].shape[0]
    for d in range(chan):
        start = pl.multiple_of(source(mine, d, chan) * rows, rows)
        obs_ref[pl.ds(start, rows), :] = parts[d][...]


def add_returned(shifts, dom, cap, nodes, blocks_ref, counts_ref, returned, total):
    me = lax.axis_index("dom")
    for d, values in zip(shifts, returned):
        q = target(me, d, dom)
        for s in range(cap):
            value = values[s].astype(F32)
            value = jnp.where(s < counts_ref[q], value, jnp.zeros_like(value))
            total[jnp.clip(blocks_ref[s, q], 0, nodes - 1)] += value


def final_kernel(dom, cap, blk, nodes, blocks_ref, counts_ref, local_ref, *rest):
    returned, (grad_ref, total) = rest[:dom], rest[dom:]
    total[...] = local_ref[:nodes]
    add_returned(range(dom), dom, cap, nodes, blocks_ref, counts_ref, returned, total)
    for k in range(nodes):
        grad_ref[:, k * blk : (k + 1) * blk] = total[k].astype(BF16)


def after(value, *others):
    return lax.optimization_barrier((value, *others))[0]


def on_device(
    latent, edge_weight, send_blocks, send_counts, edge_src, edge_obs, w_in, bias, w_out, g_out
):
    dom = lax.axis_size("dom")
    chan = lax.axis_size("chan")
    feat, cols = latent.shape
    edges, blk, _ = edge_weight.shape
    nodes = cols // blk
    cap = send_blocks.shape[1]
    obs_rows, out_width = g_out.shape
    obs = obs_rows // blk
    rows = obs_rows // chan
    hidden_width = w_in.shape[1]
    shape = jax.ShapeDtypeStruct
    plan = Plan(edges)
    near = [d for d in range(dom) if is_near(d, dom)]
    far = [d for d in range(dom) if not is_near(d, dom)]
    tables = (send_blocks.T, send_counts)
    i32 = jnp.int32

    outgoing = pl.pallas_call(
        functools.partial(pack_kernel, dom, cap, blk, nodes),
        out_shape=[shape((cap, feat, blk), BF16)] * dom,
        in_specs=hbm(3),
        out_specs=vmem(dom),
        scratch_shapes=[
            pltpu.SMEM((cap, dom), i32),
            pltpu.SMEM((dom,), i32),
            pltpu.VMEM((feat, cols), BF16),
            pltpu.SemaphoreType.DMA((3,)),
        ],
        compiler_params=params(),
        name="pack",
    )(*in_hbm(*tables, latent))
    arrived = {0: outgoing[0]}
    for d in near[1:] + far:
        arrived[d] = send(outgoing[d], "dom", d, dom)
    weights = {0: after(w_in, outgoing[0])}
    late = chan // 2 if chan & (chan - 1) == 0 else 0
    if late:
        weights[late] = send(weights[0], "chan", late, chan)
    else:
        for d in range(1, chan):
            weights[d] = send(weights[0], "chan", d, chan)

    pool = pltpu.VMEM((dom * cap + 1, blk, feat), BF16)
    first_sum, table, weight = pl.pallas_call(
        functools.partial(first_forward_kernel, plan, near, dom, cap, blk, nodes, obs),
        out_shape=[
            shape((obs + 1, blk, feat), F32),
            shape((plan.size(),), i32),
            shape(edge_weight.shape, BF16),
        ],
        in_specs=hbm(4) + vmem(len(near)),
        out_specs=vmem(1) + smem(1) + vmem(1),
        scratch_shapes=[
            pltpu.SMEM((edges,), i32),
            pltpu.SMEM((edges,), i32),
            pltpu.VMEM((feat, cols), BF16),
            pltpu.VMEM((nodes + 1, blk, feat), BF16),
            pool,
            pltpu.SemaphoreType.DMA((4,)),
        ],
        compiler_params=params(),
        cost_estimate=cost(edges),
        name="first_forward",
    )(*in_hbm(edge_src, edge_obs, latent, edge_weight), *[arrived[d] for d in near])

    shares = pl.pallas_call(
        functools.partial(far_forward_kernel, plan, far, dom, cap, chan),
        out_shape=[shape((rows, feat), BF16)] * chan,
        in_specs=smem(1) + vmem(2 + len(far)),
        out_specs=vmem(chan),
        scratch_shapes=[pool, pltpu.VMEM((obs + 1, blk, feat), F32)],
        compiler_params=params(),
        name="far_forward",
    )(table, first_sum, weight, *[arrived[d] for d in far])
    if late:
        weights[0] = after(weights[0], first_sum)
        weights[late] = after(weights[late], shares[0])
        bit = late // 2
        while bit:
            for d in sorted(weights):
                weights[d | bit] = send(weights[d], "chan", bit, chan)
            bit //= 2
    shares = [shares[0]] + [send(shares[d], "chan", d, chan) for d in range(1, chan)]

    mlp = pl.pallas_call(
        functools.partial(mlp_kernel, chan, min(512, hidden_width)),
        out_shape=[shape((rows, out_width), BF16)] + [shape((feat, rows), BF16)] * chan,
        in_specs=vmem(3 + 2 * chan),
        out_specs=vmem(1 + chan),
        scratch_shapes=[
            pltpu.VMEM((chan * feat, hidden_width), BF16),
            pltpu.VMEM((rows, chan * feat), BF16),
            pltpu.VMEM((rows, hidden_width), BF16),
        ],
        compiler_params=params(),
        name="mlp",
    )(bias.reshape(1, hidden_width), w_out, g_out, *shares, *[weights[d] for d in range(chan)])
    obs_part, grads = mlp[0], mlp[1:]
    grads = [grads[0]] + [send_back(grads[d], "chan", d, chan) for d in range(1, chan)]

    slots = pltpu.VMEM((dom * cap + 1, feat, blk), F32)
    slot_shape = shape((cap, feat, blk), BF16)
    rows_grad, *far_grads = pl.pallas_call(
        functools.partial(far_backward_kernel, plan, far, dom, cap, chan, blk, obs),
        out_shape=[shape((obs + 1, feat, blk), BF16)] + [slot_shape] * len(far),
        in_specs=smem(1) + vmem(1 + chan),
        out_specs=vmem(1 + len(far)),
        scratch_shapes=[slots],
        compiler_params=params(),
        name="far_backward",
    )(table, weight, *grads)
    returned = {d: send_back(value, "dom", d, dom) for d, value in zip(far, far_grads)}
    obs_part = after(obs_part, rows_grad)
    obs_parts = [obs_part, send(obs_part, "chan", 1, chan)]

    *near_grads, local_grad = pl.pallas_call(
        functools.partial(rest_backward_kernel, plan, near, dom, cap),
        out_shape=[slot_shape] * len(near) + [shape((nodes + 1, feat, blk), F32)],
        in_specs=smem(1) + vmem(2),
        out_specs=vmem(len(near) + 1),
        scratch_shapes=[slots],
        compiler_params=params(),
        cost_estimate=cost(edges),
        name="rest_backward",
    )(table, weight, after(rows_grad, obs_parts[1]))
    returned[0] = near_grads[0]
    for d, value in zip(near[1:], near_grads[1:]):
        returned[d] = send_back(value, "dom", d, dom)

    obs_part = after(obs_part, local_grad)
    obs_parts += [send(obs_part, "chan", d, chan) for d in range(2, chan)]
    obs_out = pl.pallas_call(
        functools.partial(rows_kernel, chan),
        out_shape=shape((obs_rows, out_width), BF16),
        in_specs=vmem(chan),
        out_specs=pl.BlockSpec(memory_space=pltpu.VMEM),
        compiler_params=params(),
        name="rows",
    )(*obs_parts)

    d_latent = pl.pallas_call(
        functools.partial(final_kernel, dom, cap, blk, nodes),
        out_shape=shape((feat, cols), BF16),
        in_specs=smem(2) + vmem(1 + dom),
        out_specs=pl.BlockSpec(memory_space=pltpu.VMEM),
        scratch_shapes=[pltpu.VMEM((nodes, feat, blk), F32)],
        compiler_params=params(),
        name="final",
    )(*tables, local_grad, *[returned[d] for d in range(dom)])
    return obs_out, d_latent


def solution(mesh):
    return jax.shard_map(
        on_device,
        mesh=mesh,
        in_specs=(
            P("chan", "dom"),
            P("dom", None, None),
            P("dom", None),
            P("dom"),
            P("dom"),
            P("dom"),
            P("chan", None),
            P(),
            P(),
            P("dom", None),
        ),
        out_specs=(P("dom", None), P("chan", "dom")),
        check_vma=False,
    )
```

```python
import functools

import jax
import jax.numpy as jnp
from jax import lax
from jax.experimental import pallas as pl
from jax.experimental.pallas import tpu as pltpu
from jax.sharding import PartitionSpec as P

F32 = jnp.float32
BF16 = jnp.bfloat16
UNROLL = 32
NT = (((1,), (1,)), ((), ()))
NN = (((1,), (0,)), ((), ()))


def target(index, shift, count):
    if count & (count - 1) == 0:
        return index ^ shift
    return (index + shift) % count


def source(index, shift, count):
    if count & (count - 1) == 0:
        return index ^ shift
    return (index + count - shift) % count


def send(value, axis, shift, count):
    return lax.ppermute(value, axis, [(i, target(i, shift, count)) for i in range(count)])


def send_back(value, axis, shift, count):
    return lax.ppermute(value, axis, [(target(i, shift, count), i) for i in range(count)])


def vmem(count):
    return [pl.BlockSpec(memory_space=pltpu.VMEM)] * count


def smem(count):
    return [pl.BlockSpec(memory_space=pltpu.SMEM)] * count


def hbm(count):
    return [pl.BlockSpec(memory_space=pltpu.HBM)] * count


def in_hbm(*values):
    return [pltpu.with_memory_space_constraint(v, pltpu.HBM) for v in values]


def cost(products):
    return pl.CostEstimate(flops=products * 2**24, bytes_accessed=2**10, transcendentals=0)


def params():
    return pltpu.CompilerParams(vmem_limit_bytes=48 * 1024 * 1024)


def is_near(shift, dom):
    return shift < (dom + 1) // 2


def fetch(pairs, sems):
    copies = [pltpu.make_async_copy(a, b, sems.at[i]) for i, (a, b) in enumerate(pairs)]
    for copy in copies:
        copy.start()
    return copies


def pack_kernel(dom, cap, blk, nodes, blocks_hbm, counts_hbm, latent_hbm, *rest):
    outs, (blocks_ref, counts_ref, latent_ref, sems) = rest[:dom], rest[dom:]
    pairs = ((latent_hbm, latent_ref), (blocks_hbm, blocks_ref), (counts_hbm, counts_ref))
    for copy in fetch(pairs, sems):
        copy.wait()
    me = lax.axis_index("dom")
    for d in range(dom):
        q = target(me, d, dom)
        for s in range(cap):
            block = jnp.clip(blocks_ref[s, q], 0, nodes - 1)
            value = latent_ref[:, pl.ds(pl.multiple_of(block * blk, blk), blk)]
            outs[d][s] = jnp.where(s < counts_ref[q], value, jnp.zeros_like(value))


class Plan:
    def __init__(self, edges):
        self.edges = edges
        self.length = edges + UNROLL

    def size(self):
        return 9 * self.length + 3

    def at(self, kind, field):
        return (kind * 3 + field) * self.length

    def make(self, ref, src_ref, obs_ref, nodes, obs, dom, cap):
        me = lax.axis_index("dom")
        mask = None
        if dom * cap <= 31:
            bits = (1 << cap) - 1
            mask = sum(bits << (source(me, d, dom) * cap) for d in range(dom) if is_near(d, dom))

        def one(e, counts):
            src = src_ref[e]
            slot = jnp.maximum(src - nodes, 0)
            if mask is not None:
                near = lax.shift_right_logical(mask, slot) & 1
            else:
                shift = lax.rem(me - lax.div(slot, cap) + dom, dom)
                near = is_near(shift, dom).astype(jnp.int32)
            local = (src < nodes).astype(jnp.int32)
            near = (1 - local) * near
            far = 1 - local - near
            kind = near + 2 * far
            i = local * counts[0] + near * counts[1] + far * counts[2]
            base = kind * 3 * self.length + i
            ref[base] = e
            ref[base + self.length] = jnp.where(local == 1, src, slot)
            ref[base + 2 * self.length] = obs_ref[e]
            return counts[0] + local, counts[1] + near, counts[2] + far

        zero = jnp.int32(0)
        counts = lax.fori_loop(0, self.edges, one, (zero, zero, zero), unroll=4)
        for kind in range(3):
            trash = nodes if kind == 0 else dom * cap
            start = counts[kind]

            def fill(i, carry):
                base = kind * 3 * self.length + start + i
                ref[base] = 0
                ref[base + self.length] = trash
                ref[base + 2 * self.length] = obs
                return carry

            lax.fori_loop(0, UNROLL, fill, 0, unroll=4)
            ref[9 * self.length + kind] = start

    def run(self, ref, kind, body):
        def step(t, carry):
            for u in range(UNROLL):
                i = kind * 3 * self.length + t * UNROLL + u
                body(ref[i], ref[i + self.length], ref[i + 2 * self.length])
            return carry

        count = ref[9 * self.length + kind]
        lax.fori_loop(0, (count + UNROLL - 1) // UNROLL, step, 0)


def first_forward_kernel(
    plan, shifts, dom, cap, blk, nodes, obs, src_hbm, obs_hbm, latent_hbm, weight_hbm, *rest
):
    count = len(shifts)
    arrived, (sum_ref, plan_ref, weight_ref) = rest[:count], rest[count : count + 3]
    src_ref, obs_ref, latent_ref, pool, slots, sems = rest[count + 3 :]
    pairs = (
        (src_hbm, src_ref),
        (obs_hbm, obs_ref),
        (latent_hbm, latent_ref),
        (weight_hbm, weight_ref),
    )
    copies = fetch(pairs, sems)
    sum_ref[...] = jnp.zeros_like(sum_ref)
    copies[0].wait()
    copies[1].wait()
    plan.make(plan_ref, src_ref, obs_ref, nodes, obs, dom, cap)
    copies[2].wait()
    for k in range(nodes):
        pool[k] = latent_ref[:, k * blk : (k + 1) * blk].T
    copies[3].wait()

    def body(e, k, j):
        sum_ref[j] += lax.dot_general(weight_ref[e], pool[k], NN, preferred_element_type=F32)

    plan.run(plan_ref, 0, body)
    add_slots(plan, 1, shifts, dom, cap, plan_ref, weight_ref, arrived, slots, sum_ref)


def add_slots(plan, kind, shifts, dom, cap, plan_ref, weight_ref, arrived, pool, total):
    me = lax.axis_index("dom")
    for d, value in zip(shifts, arrived):
        start = source(me, d, dom) * cap
        for s in range(cap):
            pool[start + s] = value[s].T

    def body(e, k, j):
        total[j] += lax.dot_general(weight_ref[e], pool[k], NN, preferred_element_type=F32)

    plan.run(plan_ref, kind, body)


def far_forward_kernel(plan, shifts, dom, cap, chan, plan_ref, sum_ref, weight_ref, *rest):
    count = len(shifts)
    arrived, outs, (pool, total) = rest[:count], rest[count : count + chan], rest[count + chan :]
    total[...] = sum_ref[...]
    add_slots(plan, 2, shifts, dom, cap, plan_ref, weight_ref, arrived, pool, total)
    whole = total.reshape(total.shape[0] * total.shape[1], total.shape[2])
    rows = outs[0].shape[0]
    mine = lax.axis_index("chan")
    for d in range(chan):
        start = pl.multiple_of(target(mine, d, chan) * rows, rows)
        outs[d][...] = whole[pl.ds(start, rows), :].astype(BF16)


def mlp_kernel(chan, tile, bias_ref, w_out_ref, g_ref, *rest):
    shares, weights = rest[:chan], rest[chan : 2 * chan]
    obs_ref, outs, (full_w, full_a, grad) = (
        rest[2 * chan],
        rest[2 * chan + 1 : 3 * chan + 1],
        rest[3 * chan + 1 :],
    )
    rows, feat = shares[0].shape
    hidden_width = grad.shape[1]
    for d in range(chan):
        full_w[d * feat : (d + 1) * feat, :] = weights[d][...]
        full_a[:, d * feat : (d + 1) * feat] = shares[d][...]
    mine = lax.axis_index("chan")
    g = g_ref[pl.ds(pl.multiple_of(mine * rows, rows), rows), :]
    out = jnp.zeros(obs_ref.shape, F32)
    for h in range(0, hidden_width, tile):
        cols = slice(h, h + tile)
        pre = lax.dot_general(full_a[...], full_w[:, cols], NN, preferred_element_type=F32)
        pre = pre + bias_ref[:, cols]
        sig = 0.5 * jnp.tanh(0.5 * pre) + 0.5
        hidden = (pre * sig).astype(BF16)
        w_out = w_out_ref[cols, :]
        out += lax.dot_general(hidden, w_out, NN, preferred_element_type=F32)
        back = lax.dot_general(g, w_out, NT, preferred_element_type=F32)
        grad[:, cols] = (back * sig * (1.0 + pre * (1.0 - sig))).astype(BF16)
    obs_ref[...] = out.astype(BF16)
    grad_agg = lax.dot_general(full_w[...], grad[...], NT, preferred_element_type=F32)
    for d in range(chan):
        outs[d][...] = grad_agg[d * feat : (d + 1) * feat].astype(BF16)


def gather_grad(chan, per, blk, shares, rows_grad):
    mine = lax.axis_index("chan")
    rows = shares[0].shape[1]
    for d in range(chan):
        start = target(mine, d, chan)
        if rows >= blk:
            for k in range(per):
                rows_grad[start * per + k] = shares[d][:, k * blk : (k + 1) * blk]
        else:
            split = blk // rows
            for k in range(split):

                @pl.when(start % split == k)
                def _():
                    rows_grad[start // split, :, k * rows : (k + 1) * rows] = shares[d][...]


def slot_backward_kernel(plan, dom, cap, chan, blk, obs, plan_ref, weight_ref, *rest):
    shares, rows_grad, (*outs, total) = rest[:chan], rest[chan], rest[chan + 1 :]
    gather_grad(chan, max(1, obs // chan), blk, shares, rows_grad)
    total[...] = jnp.zeros_like(total)

    def body(e, k, j):
        total[k] += lax.dot_general(rows_grad[j], weight_ref[e], NN, preferred_element_type=F32)

    plan.run(plan_ref, 1, body)
    plan.run(plan_ref, 2, body)
    me = lax.axis_index("dom")
    for d in range(dom):
        outs[d][...] = total[pl.ds(source(me, d, dom) * cap, cap)].astype(BF16)


def local_backward_kernel(plan, plan_ref, weight_ref, rows_grad, total):
    total[...] = jnp.zeros_like(total)

    def body(e, k, j):
        total[k] += lax.dot_general(rows_grad[j], weight_ref[e], NN, preferred_element_type=F32)

    plan.run(plan_ref, 0, body)


def rows_kernel(chan, *rest):
    parts, obs_ref = rest[:chan], rest[chan]
    mine = lax.axis_index("chan")
    rows = parts[0].shape[0]
    for d in range(chan):
        start = pl.multiple_of(source(mine, d, chan) * rows, rows)
        obs_ref[pl.ds(start, rows), :] = parts[d][...]


def add_returned(shifts, dom, cap, nodes, blocks_ref, counts_ref, returned, total):
    me = lax.axis_index("dom")
    for d, values in zip(shifts, returned):
        q = target(me, d, dom)
        for s in range(cap):
            value = values[s].astype(F32)
            value = jnp.where(s < counts_ref[q], value, jnp.zeros_like(value))
            total[jnp.clip(blocks_ref[s, q], 0, nodes - 1)] += value


def final_kernel(dom, cap, blk, nodes, blocks_ref, counts_ref, local_ref, *rest):
    returned, (grad_ref, total) = rest[:dom], rest[dom:]
    total[...] = local_ref[:nodes]
    add_returned(range(dom), dom, cap, nodes, blocks_ref, counts_ref, returned, total)
    for k in range(nodes):
        grad_ref[:, k * blk : (k + 1) * blk] = total[k].astype(BF16)


def after(value, *others):
    return lax.optimization_barrier((value, *others))[0]


def on_device(
    latent, edge_weight, send_blocks, send_counts, edge_src, edge_obs, w_in, bias, w_out, g_out
):
    dom = lax.axis_size("dom")
    chan = lax.axis_size("chan")
    feat, cols = latent.shape
    edges, blk, _ = edge_weight.shape
    nodes = cols // blk
    cap = send_blocks.shape[1]
    obs_rows, out_width = g_out.shape
    obs = obs_rows // blk
    rows = obs_rows // chan
    hidden_width = w_in.shape[1]
    shape = jax.ShapeDtypeStruct
    plan = Plan(edges)
    near = [d for d in range(dom) if is_near(d, dom)]
    far = [d for d in range(dom) if not is_near(d, dom)]
    tables = (send_blocks.T, send_counts)
    i32 = jnp.int32

    outgoing = pl.pallas_call(
        functools.partial(pack_kernel, dom, cap, blk, nodes),
        out_shape=[shape((cap, feat, blk), BF16)] * dom,
        in_specs=hbm(3),
        out_specs=vmem(dom),
        scratch_shapes=[
            pltpu.SMEM((cap, dom), i32),
            pltpu.SMEM((dom,), i32),
            pltpu.VMEM((feat, cols), BF16),
            pltpu.SemaphoreType.DMA((3,)),
        ],
        compiler_params=params(),
        name="pack",
    )(*in_hbm(*tables, latent))
    arrived = {0: outgoing[0]}
    for d in near[1:] + far:
        arrived[d] = send(outgoing[d], "dom", d, dom)
    weights = {0: after(w_in, outgoing[0])}
    late = chan // 2 if chan & (chan - 1) == 0 else 0
    if late:
        weights[late] = send(weights[0], "chan", late, chan)
    else:
        for d in range(1, chan):
            weights[d] = send(weights[0], "chan", d, chan)

    pool = pltpu.VMEM((dom * cap + 1, blk, feat), BF16)
    first_sum, table, weight = pl.pallas_call(
        functools.partial(first_forward_kernel, plan, near, dom, cap, blk, nodes, obs),
        out_shape=[
            shape((obs + 1, blk, feat), F32),
            shape((plan.size(),), i32),
            shape(edge_weight.shape, BF16),
        ],
        in_specs=hbm(4) + vmem(len(near)),
        out_specs=vmem(1) + smem(1) + vmem(1),
        scratch_shapes=[
            pltpu.SMEM((edges,), i32),
            pltpu.SMEM((edges,), i32),
            pltpu.VMEM((feat, cols), BF16),
            pltpu.VMEM((nodes + 1, blk, feat), BF16),
            pool,
            pltpu.SemaphoreType.DMA((4,)),
        ],
        compiler_params=params(),
        cost_estimate=cost(edges),
        name="first_forward",
    )(*in_hbm(edge_src, edge_obs, latent, edge_weight), *[arrived[d] for d in near])

    shares = pl.pallas_call(
        functools.partial(far_forward_kernel, plan, far, dom, cap, chan),
        out_shape=[shape((rows, feat), BF16)] * chan,
        in_specs=smem(1) + vmem(2 + len(far)),
        out_specs=vmem(chan),
        scratch_shapes=[pool, pltpu.VMEM((obs + 1, blk, feat), F32)],
        compiler_params=params(),
        name="far_forward",
    )(table, first_sum, weight, *[arrived[d] for d in far])
    if late:
        weights[0] = after(weights[0], first_sum)
        weights[late] = after(weights[late], shares[0])
        bit = late // 2
        while bit:
            for d in sorted(weights):
                weights[d | bit] = send(weights[d], "chan", bit, chan)
            bit //= 2
    shares = {d: send(shares[d], "chan", d, chan) if d else shares[0] for d in reversed(range(chan))}

    mlp = pl.pallas_call(
        functools.partial(mlp_kernel, chan, min(512, hidden_width)),
        out_shape=[shape((rows, out_width), BF16)] + [shape((feat, rows), BF16)] * chan,
        in_specs=vmem(3 + 2 * chan),
        out_specs=vmem(1 + chan),
        scratch_shapes=[
            pltpu.VMEM((chan * feat, hidden_width), BF16),
            pltpu.VMEM((rows, chan * feat), BF16),
            pltpu.VMEM((rows, hidden_width), BF16),
        ],
        compiler_params=params(),
        name="mlp",
    )(bias.reshape(1, hidden_width), w_out, g_out, *[shares[d] for d in range(chan)], *[weights[d] for d in range(chan)])
    obs_part, grads = mlp[0], mlp[1:]
    grads = {d: send_back(grads[d], "chan", d, chan) if d else grads[0] for d in reversed(range(chan))}
    obs_parts = {d: send(obs_part, "chan", d, chan) if d else obs_part for d in reversed(range(chan))}

    rows_grad, *slot_grads = pl.pallas_call(
        functools.partial(slot_backward_kernel, plan, dom, cap, chan, blk, obs),
        out_shape=[shape((obs + 1, feat, blk), BF16)] + [shape((cap, feat, blk), BF16)] * dom,
        in_specs=smem(1) + vmem(1 + chan),
        out_specs=vmem(1 + dom),
        scratch_shapes=[pltpu.VMEM((dom * cap + 1, feat, blk), F32)],
        compiler_params=params(),
        name="slot_backward",
    )(table, weight, *[grads[d] for d in range(chan)])
    returned = [slot_grads[0]] + [send_back(slot_grads[d], "dom", d, dom) for d in range(1, dom)]

    local_grad = pl.pallas_call(
        functools.partial(local_backward_kernel, plan),
        out_shape=shape((nodes + 1, feat, blk), F32),
        in_specs=smem(1) + vmem(2),
        out_specs=pl.BlockSpec(memory_space=pltpu.VMEM),
        compiler_params=params(),
        cost_estimate=cost(edges),
        name="local_backward",
    )(table, weight, rows_grad)

    obs_out = pl.pallas_call(
        functools.partial(rows_kernel, chan),
        out_shape=shape((obs_rows, out_width), BF16),
        in_specs=vmem(chan),
        out_specs=pl.BlockSpec(memory_space=pltpu.VMEM),
        compiler_params=params(),
        name="rows",
    )(*[obs_parts[d] for d in range(chan)])

    d_latent = pl.pallas_call(
        functools.partial(final_kernel, dom, cap, blk, nodes),
        out_shape=shape((feat, cols), BF16),
        in_specs=smem(2) + vmem(1 + dom),
        out_specs=pl.BlockSpec(memory_space=pltpu.VMEM),
        scratch_shapes=[pltpu.VMEM((nodes, feat, blk), F32)],
        compiler_params=params(),
        name="final",
    )(*tables, local_grad, *returned)
    return obs_out, d_latent


def solution(mesh):
    return jax.shard_map(
        on_device,
        mesh=mesh,
        in_specs=(
            P("chan", "dom"),
            P("dom", None, None),
            P("dom", None),
            P("dom"),
            P("dom"),
            P("dom"),
            P("chan", None),
            P(),
            P(),
            P("dom", None),
        ),
        out_specs=(P("dom", None), P("chan", "dom")),
        check_vma=False,
    )
```

```python
import functools

import jax
import jax.numpy as jnp
from jax import lax
from jax.experimental import pallas as pl
from jax.experimental.pallas import tpu as pltpu
from jax.sharding import PartitionSpec as P

F32 = jnp.float32
BF16 = jnp.bfloat16
UNROLL = 32
NT = (((1,), (1,)), ((), ()))
NN = (((1,), (0,)), ((), ()))


def target(index, shift, count):
    if count & (count - 1) == 0:
        return index ^ shift
    return (index + shift) % count


def source(index, shift, count):
    if count & (count - 1) == 0:
        return index ^ shift
    return (index + count - shift) % count


def send(value, axis, shift, count):
    return lax.ppermute(value, axis, [(i, target(i, shift, count)) for i in range(count)])


def send_back(value, axis, shift, count):
    return lax.ppermute(value, axis, [(target(i, shift, count), i) for i in range(count)])


def vmem(count):
    return [pl.BlockSpec(memory_space=pltpu.VMEM)] * count


def smem(count):
    return [pl.BlockSpec(memory_space=pltpu.SMEM)] * count


def hbm(count):
    return [pl.BlockSpec(memory_space=pltpu.HBM)] * count


def in_hbm(*values):
    return [pltpu.with_memory_space_constraint(v, pltpu.HBM) for v in values]


def cost(products):
    return pl.CostEstimate(flops=products * 2**24, bytes_accessed=2**10, transcendentals=0)


def params():
    return pltpu.CompilerParams(vmem_limit_bytes=48 * 1024 * 1024)


def is_near(shift, dom):
    return shift < (dom + 1) // 2


def fetch(pairs, sems):
    copies = [pltpu.make_async_copy(a, b, sems.at[i]) for i, (a, b) in enumerate(pairs)]
    for copy in copies:
        copy.start()
    return copies


def pack_kernel(dom, cap, blk, nodes, blocks_hbm, counts_hbm, latent_hbm, *rest):
    outs, (blocks_ref, counts_ref, latent_ref, sems) = rest[:dom], rest[dom:]
    pairs = ((latent_hbm, latent_ref), (blocks_hbm, blocks_ref), (counts_hbm, counts_ref))
    for copy in fetch(pairs, sems):
        copy.wait()
    me = lax.axis_index("dom")
    for d in range(dom):
        q = target(me, d, dom)
        for s in range(cap):
            block = jnp.clip(blocks_ref[s, q], 0, nodes - 1)
            value = latent_ref[:, pl.ds(pl.multiple_of(block * blk, blk), blk)]
            outs[d][s] = jnp.where(s < counts_ref[q], value, jnp.zeros_like(value))


class Plan:
    LOCAL, NEAR, FAR, SLOTS = range(4)

    def __init__(self, edges):
        self.edges = edges
        self.length = edges + UNROLL

    def size(self):
        return 6 * self.length + 2

    def make(self, ref, src_ref, obs_ref, nodes, obs, dom, cap):
        me = lax.axis_index("dom")
        length, edges = self.length, self.edges
        mask = None
        if dom * cap <= 31:
            bits = (1 << cap) - 1
            mask = sum(bits << (source(me, d, dom) * cap) for d in range(dom) if is_near(d, dom))

        def put(base, e, src, block):
            ref[base] = e
            ref[base + length] = src
            ref[base + 2 * length] = block

        def one(e, counts):
            n_local, n_near = counts
            src = src_ref[e]
            slot = jnp.maximum(src - nodes, 0)
            if mask is not None:
                near = lax.shift_right_logical(mask, slot) & 1
            else:
                shift = lax.rem(me - lax.div(slot, cap) + dom, dom)
                near = is_near(shift, dom).astype(jnp.int32)
            local = (src < nodes).astype(jnp.int32)
            near = (1 - local) * near
            n_far = e - n_local - n_near
            at_slot = 3 * length + jnp.where(near == 1, n_near, edges - 1 - n_far)
            put(jnp.where(local == 1, n_local, at_slot), e, jnp.where(local == 1, src, slot), obs_ref[e])
            return n_local + local, n_near + near

        n_local, n_near = lax.fori_loop(0, edges, one, (jnp.int32(0), jnp.int32(0)), unroll=4)

        def fill(i, carry):
            put(n_local + i, 0, nodes, obs)
            put(3 * length + edges + i, 0, dom * cap, obs)
            return carry

        lax.fori_loop(0, UNROLL, fill, 0, unroll=4)
        ref[6 * length] = n_local
        ref[6 * length + 1] = n_near

    def run(self, ref, kind, body):
        length, edges = self.length, self.edges
        n_local, n_near = ref[6 * length], ref[6 * length + 1]
        n_slots = edges - n_local
        count = (n_local, n_near, n_slots - n_near, n_slots)[kind]
        base = 0 if kind == self.LOCAL else 3 * length

        def place(i):
            if kind == self.NEAR:
                return base + jnp.where(i < n_near, i, edges)
            if kind == self.FAR:
                return base + n_local + n_near + i
            if kind == self.SLOTS:
                return base + jnp.where(i < n_near, i, i + n_local)
            return i

        def step(t, carry):
            for u in range(UNROLL):
                at = place(t * UNROLL + u)
                body(ref[at], ref[at + length], ref[at + 2 * length])
            return carry

        lax.fori_loop(0, (count + UNROLL - 1) // UNROLL, step, 0)


def first_forward_kernel(
    plan, shifts, dom, cap, blk, nodes, obs, src_hbm, obs_hbm, latent_hbm, weight_hbm, *rest
):
    count = len(shifts)
    arrived, (sum_ref, plan_ref, weight_ref) = rest[:count], rest[count : count + 3]
    src_ref, obs_ref, latent_ref, pool, slots, sems = rest[count + 3 :]
    pairs = (
        (src_hbm, src_ref),
        (obs_hbm, obs_ref),
        (latent_hbm, latent_ref),
        (weight_hbm, weight_ref),
    )
    copies = fetch(pairs, sems)
    sum_ref[...] = jnp.zeros_like(sum_ref)
    copies[0].wait()
    copies[1].wait()
    plan.make(plan_ref, src_ref, obs_ref, nodes, obs, dom, cap)
    copies[2].wait()
    for k in range(nodes):
        pool[k] = latent_ref[:, k * blk : (k + 1) * blk].T
    copies[3].wait()

    def body(e, k, j):
        sum_ref[j] += lax.dot_general(weight_ref[e], pool[k], NN, preferred_element_type=F32)

    plan.run(plan_ref, plan.LOCAL, body)
    add_slots(plan, plan.NEAR, shifts, dom, cap, plan_ref, weight_ref, arrived, slots, sum_ref)


def add_slots(plan, kind, shifts, dom, cap, plan_ref, weight_ref, arrived, pool, total):
    me = lax.axis_index("dom")
    for d, value in zip(shifts, arrived):
        start = source(me, d, dom) * cap
        for s in range(cap):
            pool[start + s] = value[s].T

    def body(e, k, j):
        total[j] += lax.dot_general(weight_ref[e], pool[k], NN, preferred_element_type=F32)

    plan.run(plan_ref, kind, body)


def far_forward_kernel(plan, shifts, dom, cap, chan, plan_ref, sum_ref, weight_ref, *rest):
    count = len(shifts)
    arrived, outs, (pool, total) = rest[:count], rest[count : count + chan], rest[count + chan :]
    total[...] = sum_ref[...]
    add_slots(plan, plan.FAR, shifts, dom, cap, plan_ref, weight_ref, arrived, pool, total)
    whole = total.reshape(total.shape[0] * total.shape[1], total.shape[2])
    rows = outs[0].shape[0]
    mine = lax.axis_index("chan")
    for d in range(chan):
        start = pl.multiple_of(target(mine, d, chan) * rows, rows)
        outs[d][...] = whole[pl.ds(start, rows), :].astype(BF16)


def mlp_kernel(chan, tile, bias_ref, w_out_ref, g_ref, *rest):
    shares, weights = rest[:chan], rest[chan : 2 * chan]
    obs_ref, outs, (full_w, full_a, grad) = (
        rest[2 * chan],
        rest[2 * chan + 1 : 3 * chan + 1],
        rest[3 * chan + 1 :],
    )
    rows, feat = shares[0].shape
    hidden_width = grad.shape[1]
    for d in range(chan):
        full_w[d * feat : (d + 1) * feat, :] = weights[d][...]
        full_a[:, d * feat : (d + 1) * feat] = shares[d][...]
    mine = lax.axis_index("chan")
    g = g_ref[pl.ds(pl.multiple_of(mine * rows, rows), rows), :]
    out = jnp.zeros(obs_ref.shape, F32)
    for h in range(0, hidden_width, tile):
        cols = slice(h, h + tile)
        pre = lax.dot_general(full_a[...], full_w[:, cols], NN, preferred_element_type=F32)
        pre = pre + bias_ref[:, cols]
        sig = 0.5 * jnp.tanh(0.5 * pre) + 0.5
        hidden = (pre * sig).astype(BF16)
        w_out = w_out_ref[cols, :]
        out += lax.dot_general(hidden, w_out, NN, preferred_element_type=F32)
        back = lax.dot_general(g, w_out, NT, preferred_element_type=F32)
        grad[:, cols] = (back * sig * (1.0 + pre * (1.0 - sig))).astype(BF16)
    obs_ref[...] = out.astype(BF16)
    grad_agg = lax.dot_general(full_w[...], grad[...], NT, preferred_element_type=F32)
    for d in range(chan):
        outs[d][...] = grad_agg[d * feat : (d + 1) * feat].astype(BF16)


def gather_grad(chan, per, blk, shares, rows_grad):
    mine = lax.axis_index("chan")
    rows = shares[0].shape[1]
    for d in range(chan):
        start = target(mine, d, chan)
        if rows >= blk:
            for k in range(per):
                rows_grad[start * per + k] = shares[d][:, k * blk : (k + 1) * blk]
        else:
            split = blk // rows
            for k in range(split):

                @pl.when(start % split == k)
                def _():
                    rows_grad[start // split, :, k * rows : (k + 1) * rows] = shares[d][...]


def slot_backward_kernel(plan, dom, cap, chan, blk, obs, plan_ref, weight_ref, *rest):
    shares, rows_grad, (*outs, total) = rest[:chan], rest[chan], rest[chan + 1 :]
    gather_grad(chan, max(1, obs // chan), blk, shares, rows_grad)
    total[...] = jnp.zeros_like(total)

    def body(e, k, j):
        total[k] += lax.dot_general(rows_grad[j], weight_ref[e], NN, preferred_element_type=F32)

    plan.run(plan_ref, plan.SLOTS, body)
    me = lax.axis_index("dom")
    for d in range(dom):
        outs[d][...] = total[pl.ds(source(me, d, dom) * cap, cap)].astype(BF16)


def local_backward_kernel(plan, plan_ref, weight_ref, rows_grad, total):
    total[...] = jnp.zeros_like(total)

    def body(e, k, j):
        total[k] += lax.dot_general(rows_grad[j], weight_ref[e], NN, preferred_element_type=F32)

    plan.run(plan_ref, plan.LOCAL, body)


def rows_kernel(chan, *rest):
    parts, obs_ref = rest[:chan], rest[chan]
    mine = lax.axis_index("chan")
    rows = parts[0].shape[0]
    for d in range(chan):
        start = pl.multiple_of(source(mine, d, chan) * rows, rows)
        obs_ref[pl.ds(start, rows), :] = parts[d][...]


def add_returned(shifts, dom, cap, nodes, blocks_ref, counts_ref, returned, total):
    me = lax.axis_index("dom")
    for d, values in zip(shifts, returned):
        q = target(me, d, dom)
        for s in range(cap):
            value = values[s].astype(F32)
            value = jnp.where(s < counts_ref[q], value, jnp.zeros_like(value))
            total[jnp.clip(blocks_ref[s, q], 0, nodes - 1)] += value


def final_kernel(order, dom, cap, blk, nodes, blocks_ref, counts_ref, local_ref, *rest):
    returned, (grad_ref, total) = rest[:dom], rest[dom:]
    total[...] = local_ref[:nodes]
    add_returned(order, dom, cap, nodes, blocks_ref, counts_ref, returned, total)
    for k in range(nodes):
        grad_ref[:, k * blk : (k + 1) * blk] = total[k].astype(BF16)


def after(value, *others):
    return lax.optimization_barrier((value, *others))[0]


def on_device(
    latent, edge_weight, send_blocks, send_counts, edge_src, edge_obs, w_in, bias, w_out, g_out
):
    dom = lax.axis_size("dom")
    chan = lax.axis_size("chan")
    feat, cols = latent.shape
    edges, blk, _ = edge_weight.shape
    nodes = cols // blk
    cap = send_blocks.shape[1]
    obs_rows, out_width = g_out.shape
    obs = obs_rows // blk
    rows = obs_rows // chan
    hidden_width = w_in.shape[1]
    shape = jax.ShapeDtypeStruct
    plan = Plan(edges)
    near = [d for d in range(dom) if is_near(d, dom)]
    far = [d for d in range(dom) if not is_near(d, dom)]
    tables = (send_blocks.T, send_counts)
    i32 = jnp.int32

    outgoing = pl.pallas_call(
        functools.partial(pack_kernel, dom, cap, blk, nodes),
        out_shape=[shape((cap, feat, blk), BF16)] * dom,
        in_specs=hbm(3),
        out_specs=vmem(dom),
        scratch_shapes=[
            pltpu.SMEM((cap, dom), i32),
            pltpu.SMEM((dom,), i32),
            pltpu.VMEM((feat, cols), BF16),
            pltpu.SemaphoreType.DMA((3,)),
        ],
        compiler_params=params(),
        name="pack",
    )(*in_hbm(*tables, latent))
    arrived = {0: outgoing[0]}
    for d in near[1:] + far:
        arrived[d] = send(outgoing[d], "dom", d, dom)
    weights = {0: after(w_in, outgoing[0])}
    late = chan // 2 if chan & (chan - 1) == 0 else 0
    if late:
        weights[late] = send(weights[0], "chan", late, chan)
    else:
        for d in range(1, chan):
            weights[d] = send(weights[0], "chan", d, chan)

    pool = pltpu.VMEM((dom * cap + 1, blk, feat), BF16)
    first_sum, table, weight = pl.pallas_call(
        functools.partial(first_forward_kernel, plan, near, dom, cap, blk, nodes, obs),
        out_shape=[
            shape((obs + 1, blk, feat), F32),
            shape((plan.size(),), i32),
            shape(edge_weight.shape, BF16),
        ],
        in_specs=hbm(4) + vmem(len(near)),
        out_specs=vmem(1) + smem(1) + vmem(1),
        scratch_shapes=[
            pltpu.SMEM((edges,), i32),
            pltpu.SMEM((edges,), i32),
            pltpu.VMEM((feat, cols), BF16),
            pltpu.VMEM((nodes + 1, blk, feat), BF16),
            pool,
            pltpu.SemaphoreType.DMA((4,)),
        ],
        compiler_params=params(),
        cost_estimate=cost(edges),
        name="first_forward",
    )(*in_hbm(edge_src, edge_obs, latent, edge_weight), *[arrived[d] for d in near])

    shares = pl.pallas_call(
        functools.partial(far_forward_kernel, plan, far, dom, cap, chan),
        out_shape=[shape((rows, feat), BF16)] * chan,
        in_specs=smem(1) + vmem(2 + len(far)),
        out_specs=vmem(chan),
        scratch_shapes=[pool, pltpu.VMEM((obs + 1, blk, feat), F32)],
        compiler_params=params(),
        name="far_forward",
    )(table, first_sum, weight, *[arrived[d] for d in far])
    if late:
        weights[0] = after(weights[0], first_sum)
        weights[late] = after(weights[late], shares[0])
        bit = late // 2
        while bit:
            for d in sorted(weights):
                weights[d | bit] = send(weights[d], "chan", bit, chan)
            bit //= 2
    shares = {d: send(shares[d], "chan", d, chan) if d else shares[0] for d in reversed(range(chan))}

    mlp = pl.pallas_call(
        functools.partial(mlp_kernel, chan, min(1024, hidden_width)),
        out_shape=[shape((rows, out_width), BF16)] + [shape((feat, rows), BF16)] * chan,
        in_specs=vmem(3 + 2 * chan),
        out_specs=vmem(1 + chan),
        scratch_shapes=[
            pltpu.VMEM((chan * feat, hidden_width), BF16),
            pltpu.VMEM((rows, chan * feat), BF16),
            pltpu.VMEM((rows, hidden_width), BF16),
        ],
        compiler_params=params(),
        name="mlp",
    )(bias.reshape(1, hidden_width), w_out, g_out, *[shares[d] for d in range(chan)], *[weights[d] for d in range(chan)])
    obs_part, grads = mlp[0], mlp[1:]
    grads = {d: send_back(grads[d], "chan", d, chan) if d else grads[0] for d in reversed(range(chan))}
    obs_parts = {d: send(obs_part, "chan", d, chan) if d else obs_part for d in reversed(range(chan))}

    rows_grad, *slot_grads = pl.pallas_call(
        functools.partial(slot_backward_kernel, plan, dom, cap, chan, blk, obs),
        out_shape=[shape((obs + 1, feat, blk), BF16)] + [shape((cap, feat, blk), BF16)] * dom,
        in_specs=smem(1) + vmem(1 + chan),
        out_specs=vmem(1 + dom),
        scratch_shapes=[pltpu.VMEM((dom * cap + 1, feat, blk), F32)],
        compiler_params=params(),
        name="slot_backward",
    )(table, weight, *[grads[d] for d in range(chan)])
    returned = [slot_grads[0]] + [send_back(slot_grads[d], "dom", d, dom) for d in range(1, dom)]

    local_grad = pl.pallas_call(
        functools.partial(local_backward_kernel, plan),
        out_shape=shape((nodes + 1, feat, blk), F32),
        in_specs=smem(1) + vmem(2),
        out_specs=pl.BlockSpec(memory_space=pltpu.VMEM),
        compiler_params=params(),
        cost_estimate=cost(edges),
        name="local_backward",
    )(table, weight, rows_grad)

    obs_out = pl.pallas_call(
        functools.partial(rows_kernel, chan),
        out_shape=shape((obs_rows, out_width), BF16),
        in_specs=vmem(chan),
        out_specs=pl.BlockSpec(memory_space=pltpu.VMEM),
        compiler_params=params(),
        name="rows",
    )(*[obs_parts[d] for d in range(chan)])

    back_order = near[:2] + far[::2] + far[1::2] + near[2:]
    d_latent = pl.pallas_call(
        functools.partial(final_kernel, back_order, dom, cap, blk, nodes),
        out_shape=shape((feat, cols), BF16),
        in_specs=smem(2) + vmem(1 + dom),
        out_specs=pl.BlockSpec(memory_space=pltpu.VMEM),
        scratch_shapes=[pltpu.VMEM((nodes, feat, blk), F32)],
        compiler_params=params(),
        name="final",
    )(*tables, local_grad, *[returned[d] for d in back_order])
    return obs_out, d_latent


def solution(mesh):
    return jax.shard_map(
        on_device,
        mesh=mesh,
        in_specs=(
            P("chan", "dom"),
            P("dom", None, None),
            P("dom", None),
            P("dom"),
            P("dom"),
            P("dom"),
            P("chan", None),
            P(),
            P(),
            P("dom", None),
        ),
        out_specs=(P("dom", None), P("chan", "dom")),
        check_vma=False,
    )
```

```python
import functools

import jax
import jax.numpy as jnp
from jax import lax
from jax.experimental import pallas as pl
from jax.experimental.pallas import tpu as pltpu
from jax.sharding import PartitionSpec as P

F32 = jnp.float32
BF16 = jnp.bfloat16
UNROLL = 48
TAIL = 16
NT = (((1,), (1,)), ((), ()))
NN = (((1,), (0,)), ((), ()))


def target(index, shift, count):
    if count & (count - 1) == 0:
        return index ^ shift
    return (index + shift) % count


def source(index, shift, count):
    if count & (count - 1) == 0:
        return index ^ shift
    return (index + count - shift) % count


def send(value, axis, shift, count):
    return lax.ppermute(value, axis, [(i, target(i, shift, count)) for i in range(count)])


def send_back(value, axis, shift, count):
    return lax.ppermute(value, axis, [(target(i, shift, count), i) for i in range(count)])


def vmem(count):
    return [pl.BlockSpec(memory_space=pltpu.VMEM)] * count


def smem(count):
    return [pl.BlockSpec(memory_space=pltpu.SMEM)] * count


def hbm(count):
    return [pl.BlockSpec(memory_space=pltpu.HBM)] * count


def in_hbm(*values):
    return [pltpu.with_memory_space_constraint(v, pltpu.HBM) for v in values]


def cost(products):
    return pl.CostEstimate(flops=products * 2**24, bytes_accessed=2**10, transcendentals=0)


def params():
    return pltpu.CompilerParams(vmem_limit_bytes=48 * 1024 * 1024)


def is_near(shift, dom):
    return shift < (dom + 1) // 2


def fetch(pairs, sems):
    copies = [pltpu.make_async_copy(a, b, sems.at[i]) for i, (a, b) in enumerate(pairs)]
    for copy in copies:
        copy.start()
    return copies


def pack_kernel(dom, cap, blk, nodes, blocks_hbm, counts_hbm, latent_hbm, *rest):
    outs, (blocks_ref, counts_ref, latent_ref, sems) = rest[:dom], rest[dom:]
    pairs = ((latent_hbm, latent_ref), (blocks_hbm, blocks_ref), (counts_hbm, counts_ref))
    for copy in fetch(pairs, sems):
        copy.wait()
    me = lax.axis_index("dom")
    for d in range(dom):
        q = target(me, d, dom)
        for s in range(cap):
            block = jnp.clip(blocks_ref[s, q], 0, nodes - 1)
            value = latent_ref[:, pl.ds(pl.multiple_of(block * blk, blk), blk)]
            outs[d][s] = jnp.where(s < counts_ref[q], value, jnp.zeros_like(value))


class Plan:
    LOCAL, NEAR, FAR, SLOTS = range(4)

    def __init__(self, edges):
        self.edges = edges
        self.length = edges + UNROLL

    def size(self):
        return 6 * self.length + 2

    def make(self, ref, src_ref, obs_ref, nodes, obs, dom, cap):
        me = lax.axis_index("dom")
        length, edges = self.length, self.edges
        mask = None
        if dom * cap <= 31:
            bits = (1 << cap) - 1
            mask = sum(bits << (source(me, d, dom) * cap) for d in range(dom) if is_near(d, dom))

        def put(base, e, src, block):
            ref[base] = e
            ref[base + length] = src
            ref[base + 2 * length] = block

        def one(e, counts):
            n_local, n_near = counts
            src = src_ref[e]
            slot = jnp.maximum(src - nodes, 0)
            if mask is not None:
                near = lax.shift_right_logical(mask, slot) & 1
            else:
                shift = lax.rem(me - lax.div(slot, cap) + dom, dom)
                near = is_near(shift, dom).astype(jnp.int32)
            local = (src < nodes).astype(jnp.int32)
            near = (1 - local) * near
            n_far = e - n_local - n_near
            at_slot = 3 * length + jnp.where(near == 1, n_near, edges - 1 - n_far)
            put(jnp.where(local == 1, n_local, at_slot), e, jnp.where(local == 1, src, slot), obs_ref[e])
            return n_local + local, n_near + near

        n_local, n_near = lax.fori_loop(0, edges, one, (jnp.int32(0), jnp.int32(0)), unroll=4)

        def fill(i, carry):
            put(n_local + i, 0, nodes, obs)
            put(3 * length + edges + i, 0, dom * cap, obs)
            return carry

        lax.fori_loop(0, UNROLL, fill, 0, unroll=4)
        ref[6 * length] = n_local
        ref[6 * length + 1] = n_near

    def run(self, ref, kind, body):
        length, edges = self.length, self.edges
        n_local, n_near = ref[6 * length], ref[6 * length + 1]
        n_slots = edges - n_local
        count = (n_local, n_near, n_slots - n_near, n_slots)[kind]
        base = 0 if kind == self.LOCAL else 3 * length

        def place(i):
            if kind == self.NEAR:
                return base + jnp.where(i < n_near, i, edges)
            if kind == self.FAR:
                return base + n_local + n_near + i
            if kind == self.SLOTS:
                return base + jnp.where(i < n_near, i, i + n_local)
            return i

        def step(start, width, t, carry):
            for u in range(width):
                at = place(start + t * width + u)
                body(ref[at], ref[at + length], ref[at + 2 * length])
            return carry

        full = lax.div(count + UNROLL - 1 - TAIL, UNROLL)
        done = full * UNROLL
        left = jnp.maximum(count - done, 0)
        lax.fori_loop(0, full, functools.partial(step, 0, UNROLL), 0)
        lax.fori_loop(0, lax.div(left + TAIL - 1, TAIL), functools.partial(step, done, TAIL), 0)


def first_forward_kernel(
    plan, shifts, dom, cap, blk, nodes, obs, src_hbm, obs_hbm, latent_hbm, weight_hbm, *rest
):
    count = len(shifts)
    arrived, (sum_ref, plan_ref, weight_ref) = rest[:count], rest[count : count + 3]
    src_ref, obs_ref, latent_ref, pool, slots, sems = rest[count + 3 :]
    pairs = (
        (src_hbm, src_ref),
        (obs_hbm, obs_ref),
        (latent_hbm, latent_ref),
        (weight_hbm, weight_ref),
    )
    copies = fetch(pairs, sems)
    sum_ref[...] = jnp.zeros_like(sum_ref)
    copies[0].wait()
    copies[1].wait()
    plan.make(plan_ref, src_ref, obs_ref, nodes, obs, dom, cap)
    copies[2].wait()
    for k in range(nodes):
        pool[k] = latent_ref[:, k * blk : (k + 1) * blk].T
    copies[3].wait()

    def body(e, k, j):
        sum_ref[j] += lax.dot_general(weight_ref[e], pool[k], NN, preferred_element_type=F32)

    plan.run(plan_ref, plan.LOCAL, body)
    add_slots(plan, plan.NEAR, shifts, dom, cap, plan_ref, weight_ref, arrived, slots, sum_ref)


def add_slots(plan, kind, shifts, dom, cap, plan_ref, weight_ref, arrived, pool, total):
    me = lax.axis_index("dom")
    for d, value in zip(shifts, arrived):
        start = source(me, d, dom) * cap
        for s in range(cap):
            pool[start + s] = value[s].T

    def body(e, k, j):
        total[j] += lax.dot_general(weight_ref[e], pool[k], NN, preferred_element_type=F32)

    plan.run(plan_ref, kind, body)


def far_forward_kernel(plan, shifts, dom, cap, chan, plan_ref, sum_ref, weight_ref, *rest):
    count = len(shifts)
    arrived, outs, (pool, total) = rest[:count], rest[count : count + chan], rest[count + chan :]
    total[...] = sum_ref[...]
    add_slots(plan, plan.FAR, shifts, dom, cap, plan_ref, weight_ref, arrived, pool, total)
    whole = total.reshape(total.shape[0] * total.shape[1], total.shape[2])
    rows = outs[0].shape[0]
    mine = lax.axis_index("chan")
    for d in range(chan):
        start = pl.multiple_of(target(mine, d, chan) * rows, rows)
        outs[d][...] = whole[pl.ds(start, rows), :].astype(BF16)


def mlp_kernel(chan, tile, bias_ref, w_out_ref, g_ref, *rest):
    shares, weights = rest[:chan], rest[chan : 2 * chan]
    obs_ref, outs, (full_w, full_a, grad) = (
        rest[2 * chan],
        rest[2 * chan + 1 : 3 * chan + 1],
        rest[3 * chan + 1 :],
    )
    rows, feat = shares[0].shape
    hidden_width = grad.shape[1]
    for d in range(chan):
        full_w[d * feat : (d + 1) * feat, :] = weights[d][...]
        full_a[:, d * feat : (d + 1) * feat] = shares[d][...]
    mine = lax.axis_index("chan")
    g = g_ref[pl.ds(pl.multiple_of(mine * rows, rows), rows), :]
    out = jnp.zeros(obs_ref.shape, F32)
    for h in range(0, hidden_width, tile):
        cols = slice(h, h + tile)
        pre = lax.dot_general(full_a[...], full_w[:, cols], NN, preferred_element_type=F32)
        pre = pre + bias_ref[:, cols]
        sig = 0.5 * jnp.tanh(0.5 * pre) + 0.5
        hidden = (pre * sig).astype(BF16)
        w_out = w_out_ref[cols, :]
        out += lax.dot_general(hidden, w_out, NN, preferred_element_type=F32)
        back = lax.dot_general(g, w_out, NT, preferred_element_type=F32)
        grad[:, cols] = (back * sig * (1.0 + pre * (1.0 - sig))).astype(BF16)
    obs_ref[...] = out.astype(BF16)
    grad_agg = lax.dot_general(full_w[...], grad[...], NT, preferred_element_type=F32)
    for d in range(chan):
        outs[d][...] = grad_agg[d * feat : (d + 1) * feat].astype(BF16)


def gather_grad(chan, per, blk, shares, rows_grad):
    mine = lax.axis_index("chan")
    rows = shares[0].shape[1]
    for d in range(chan):
        start = target(mine, d, chan)
        if rows >= blk:
            for k in range(per):
                rows_grad[start * per + k] = shares[d][:, k * blk : (k + 1) * blk]
        else:
            split = blk // rows
            for k in range(split):

                @pl.when(start % split == k)
                def _():
                    rows_grad[start // split, :, k * rows : (k + 1) * rows] = shares[d][...]


def slot_backward_kernel(plan, dom, cap, chan, blk, obs, plan_ref, weight_ref, *rest):
    shares, rows_grad, (*outs, total) = rest[:chan], rest[chan], rest[chan + 1 :]
    gather_grad(chan, max(1, obs // chan), blk, shares, rows_grad)
    total[...] = jnp.zeros_like(total)

    def body(e, k, j):
        total[k] += lax.dot_general(rows_grad[j], weight_ref[e], NN, preferred_element_type=F32)

    plan.run(plan_ref, plan.SLOTS, body)
    me = lax.axis_index("dom")
    for d in range(dom):
        outs[d][...] = total[pl.ds(source(me, d, dom) * cap, cap)].astype(BF16)


def local_backward_kernel(plan, plan_ref, weight_ref, rows_grad, total):
    total[...] = jnp.zeros_like(total)

    def body(e, k, j):
        total[k] += lax.dot_general(rows_grad[j], weight_ref[e], NN, preferred_element_type=F32)

    plan.run(plan_ref, plan.LOCAL, body)


def rows_kernel(chan, *rest):
    parts, obs_ref = rest[:chan], rest[chan]
    mine = lax.axis_index("chan")
    rows = parts[0].shape[0]
    for d in range(chan):
        start = pl.multiple_of(source(mine, d, chan) * rows, rows)
        obs_ref[pl.ds(start, rows), :] = parts[d][...]


def add_returned(shifts, dom, cap, nodes, blocks_ref, counts_ref, returned, total):
    me = lax.axis_index("dom")
    for d, values in zip(shifts, returned):
        q = target(me, d, dom)
        for s in range(cap):
            value = values[s].astype(F32)
            value = jnp.where(s < counts_ref[q], value, jnp.zeros_like(value))
            total[jnp.clip(blocks_ref[s, q], 0, nodes - 1)] += value


def final_kernel(order, dom, cap, blk, nodes, blocks_ref, counts_ref, local_ref, *rest):
    returned, (grad_ref, total) = rest[:dom], rest[dom:]
    total[...] = local_ref[:nodes]
    add_returned(order, dom, cap, nodes, blocks_ref, counts_ref, returned, total)
    for k in range(nodes):
        grad_ref[:, k * blk : (k + 1) * blk] = total[k].astype(BF16)


def after(value, *others):
    return lax.optimization_barrier((value, *others))[0]


def on_device(
    latent, edge_weight, send_blocks, send_counts, edge_src, edge_obs, w_in, bias, w_out, g_out
):
    dom = lax.axis_size("dom")
    chan = lax.axis_size("chan")
    feat, cols = latent.shape
    edges, blk, _ = edge_weight.shape
    nodes = cols // blk
    cap = send_blocks.shape[1]
    obs_rows, out_width = g_out.shape
    obs = obs_rows // blk
    rows = obs_rows // chan
    hidden_width = w_in.shape[1]
    shape = jax.ShapeDtypeStruct
    plan = Plan(edges)
    near = [d for d in range(dom) if is_near(d, dom)]
    far = [d for d in range(dom) if not is_near(d, dom)]
    tables = (send_blocks.T, send_counts)
    i32 = jnp.int32

    outgoing = pl.pallas_call(
        functools.partial(pack_kernel, dom, cap, blk, nodes),
        out_shape=[shape((cap, feat, blk), BF16)] * dom,
        in_specs=hbm(3),
        out_specs=vmem(dom),
        scratch_shapes=[
            pltpu.SMEM((cap, dom), i32),
            pltpu.SMEM((dom,), i32),
            pltpu.VMEM((feat, cols), BF16),
            pltpu.SemaphoreType.DMA((3,)),
        ],
        compiler_params=params(),
        name="pack",
    )(*in_hbm(*tables, latent))
    arrived = {0: outgoing[0]}
    for d in near[1:] + far:
        arrived[d] = send(outgoing[d], "dom", d, dom)
    weights = {0: after(w_in, outgoing[0])}
    late = chan // 2 if chan & (chan - 1) == 0 else 0
    if late:
        weights[late] = send(weights[0], "chan", late, chan)
    else:
        for d in range(1, chan):
            weights[d] = send(weights[0], "chan", d, chan)

    pool = pltpu.VMEM((dom * cap + 1, blk, feat), BF16)
    first_sum, table, weight = pl.pallas_call(
        functools.partial(first_forward_kernel, plan, near, dom, cap, blk, nodes, obs),
        out_shape=[
            shape((obs + 1, blk, feat), F32),
            shape((plan.size(),), i32),
            shape(edge_weight.shape, BF16),
        ],
        in_specs=hbm(4) + vmem(len(near)),
        out_specs=vmem(1) + smem(1) + vmem(1),
        scratch_shapes=[
            pltpu.SMEM((edges,), i32),
            pltpu.SMEM((edges,), i32),
            pltpu.VMEM((feat, cols), BF16),
            pltpu.VMEM((nodes + 1, blk, feat), BF16),
            pool,
            pltpu.SemaphoreType.DMA((4,)),
        ],
        compiler_params=params(),
        cost_estimate=cost(edges),
        name="first_forward",
    )(*in_hbm(edge_src, edge_obs, latent, edge_weight), *[arrived[d] for d in near])

    shares = pl.pallas_call(
        functools.partial(far_forward_kernel, plan, far, dom, cap, chan),
        out_shape=[shape((rows, feat), BF16)] * chan,
        in_specs=smem(1) + vmem(2 + len(far)),
        out_specs=vmem(chan),
        scratch_shapes=[pool, pltpu.VMEM((obs + 1, blk, feat), F32)],
        compiler_params=params(),
        name="far_forward",
    )(table, first_sum, weight, *[arrived[d] for d in far])
    if late:
        weights[0] = after(weights[0], first_sum)
        weights[late] = after(weights[late], shares[0])
        bit = late // 2
        while bit:
            for d in sorted(weights):
                weights[d | bit] = send(weights[d], "chan", bit, chan)
            bit //= 2
    shares = {d: send(shares[d], "chan", d, chan) if d else shares[0] for d in reversed(range(chan))}

    mlp = pl.pallas_call(
        functools.partial(mlp_kernel, chan, min(1024, hidden_width)),
        out_shape=[shape((rows, out_width), BF16)] + [shape((feat, rows), BF16)] * chan,
        in_specs=vmem(3 + 2 * chan),
        out_specs=vmem(1 + chan),
        scratch_shapes=[
            pltpu.VMEM((chan * feat, hidden_width), BF16),
            pltpu.VMEM((rows, chan * feat), BF16),
            pltpu.VMEM((rows, hidden_width), BF16),
        ],
        compiler_params=params(),
        name="mlp",
    )(bias.reshape(1, hidden_width), w_out, g_out, *[shares[d] for d in range(chan)], *[weights[d] for d in range(chan)])
    obs_part, grads = mlp[0], mlp[1:]
    grads = {d: send_back(grads[d], "chan", d, chan) if d else grads[0] for d in reversed(range(chan))}
    obs_parts = {d: send(obs_part, "chan", d, chan) if d else obs_part for d in reversed(range(chan))}

    rows_grad, *slot_grads = pl.pallas_call(
        functools.partial(slot_backward_kernel, plan, dom, cap, chan, blk, obs),
        out_shape=[shape((obs + 1, feat, blk), BF16)] + [shape((cap, feat, blk), BF16)] * dom,
        in_specs=smem(1) + vmem(1 + chan),
        out_specs=vmem(1 + dom),
        scratch_shapes=[pltpu.VMEM((dom * cap + 1, feat, blk), F32)],
        compiler_params=params(),
        name="slot_backward",
    )(table, weight, *[grads[d] for d in range(chan)])
    returned = [slot_grads[0]] + [send_back(slot_grads[d], "dom", d, dom) for d in range(1, dom)]

    local_grad = pl.pallas_call(
        functools.partial(local_backward_kernel, plan),
        out_shape=shape((nodes + 1, feat, blk), F32),
        in_specs=smem(1) + vmem(2),
        out_specs=pl.BlockSpec(memory_space=pltpu.VMEM),
        compiler_params=params(),
        cost_estimate=cost(edges),
        name="local_backward",
    )(table, weight, rows_grad)

    obs_out = pl.pallas_call(
        functools.partial(rows_kernel, chan),
        out_shape=shape((obs_rows, out_width), BF16),
        in_specs=vmem(chan),
        out_specs=pl.BlockSpec(memory_space=pltpu.VMEM),
        compiler_params=params(),
        name="rows",
    )(*[obs_parts[d] for d in range(chan)])

    back_order = near[:2] + far[::2] + far[1::2] + near[2:]
    d_latent = pl.pallas_call(
        functools.partial(final_kernel, back_order, dom, cap, blk, nodes),
        out_shape=shape((feat, cols), BF16),
        in_specs=smem(2) + vmem(1 + dom),
        out_specs=pl.BlockSpec(memory_space=pltpu.VMEM),
        scratch_shapes=[pltpu.VMEM((nodes, feat, blk), F32)],
        compiler_params=params(),
        name="final",
    )(*tables, local_grad, *[returned[d] for d in back_order])
    return obs_out, d_latent


def solution(mesh):
    return jax.shard_map(
        on_device,
        mesh=mesh,
        in_specs=(
            P("chan", "dom"),
            P("dom", None, None),
            P("dom", None),
            P("dom"),
            P("dom"),
            P("dom"),
            P("chan", None),
            P(),
            P(),
            P("dom", None),
        ),
        out_specs=(P("dom", None), P("chan", "dom")),
        check_vma=False,
    )
```
